256 devices in a mesh: gx: 8 (over z), gy: 4 (over y_lo, core), gz: 8 (over x, y_hi).
Axes of the slice: x: 4, y: 4 (y_hi: 2, y_lo: 2; y = y_hi * 2 + y_lo), z: 8, core: 2. Of those that a mesh axis runs over, the one named last changes fastest.
Arguments:
- features: bfloat16 [64, 16, 32, 1024], P(None, 'gx', 'gy', 'gz'), may hold values from -6 to 6
- dest_bricks: int32 [8192, 1], P(('gx', 'gy', 'gz')), may hold values from 0 to 31
- cell_ids: int32 [8192, 64], P(('gx', 'gy', 'gz')), may hold values from 0 to 2047
- cic_masses: bfloat16 [8192, 64], P(('gx', 'gy', 'gz')), may hold values from 0.25 to 4
- live_counts: int32 [256], P(('gx', 'gy', 'gz')), may hold values from 8 to 32
- style_vector: float32 [512], replicated, may hold values from -6 to 6
- affine_first: float32 [512, 64], replicated, may hold values from -0.25 to 0.25
- kernel_first: bfloat16 [27, 64, 64], replicated, may hold values from -0.15625 to 0.15625
- bias_first: float32 [64], replicated, may hold values from -0.5 to 0.5
- gain_first: float32 [64], replicated, may hold values from 1 to 4
- affine_second: float32 [512, 64], replicated, may hold values from -0.25 to 0.25
- kernel_second: bfloat16 [27, 64, 64], replicated, may hold values from -0.15625 to 0.15625
- bias_second: float32 [64], replicated, may hold values from -0.5 to 0.5
- gain_second: float32 [64], replicated, may hold values from 1 to 4
Outputs:
- upsampled: bfloat16 [64, 16, 32, 1024], P(None, 'gx', 'gy', 'gz')
The draws below stay inside these ranges and needn't reach their ends.
All inputs are finite; a program needn't handle non-finite values.
Results may differ from the reference program's by a relative error of at most 0.0054.
Values may be sent and summed in bfloat16 or wider, within the bound.
A program may use at most 64 MiB of HBM per device.

```python
import math
import jax
import jax.numpy as jnp
from jax import lax

C = 64
STYLE = 512
BX = 2
BY = 8
BZ = 128
NB = 32
PB = 64
CELLS = 2048
GROUP = 32
BLOCKS = 8192
NX = 16
NY = 32
NZ = 1024
N_GX = 8
N_GY = 4
N_GZ = 8
DEVICES = 256


def with_ends(entries, key, least, high):
    longest = entries.shape.index(max(entries.shape))
    spots = []
    for shift in (0, 1):
        where = [jax.random.randint(jax.random.fold_in(key, axis), (), 0, length) for axis, length in enumerate(entries.shape)]
        where[longest] = (where[longest] + shift) % entries.shape[longest]
        spots.append(tuple(where))
    return entries.at[spots[0]].set(least).at[spots[1]].set(high)


def level_of(own_key, shape, split, smallest, high):
    level = 1.0
    for axis_at, parts in split:
        steps = jax.random.uniform(jax.random.fold_in(jax.random.fold_in(own_key, 6), axis_at), (parts,), jnp.float32, smallest / len(split), high / len(split))
        level = level * jnp.repeat(jnp.exp(steps), shape[axis_at] // parts).reshape((-1,) + (1,) * (len(shape) - 1 - axis_at))
    return level


def different_ones(rng, rows, amount, top, lift):
    order = jax.random.permutation(jax.random.fold_in(rng, 1), amount)
    boost = order
    for power in range(3):
        boost = boost * boost // amount
    boost = boost * lift // amount
    lots = jax.random.randint(jax.random.fold_in(rng, 2), (rows, amount), 0, 4096) + boost
    holders = jax.random.permutation(jax.random.fold_in(rng, 3), rows)[jnp.arange(amount) % rows]
    lots = jnp.where(jnp.arange(rows)[:, None] == holders[None, :], 1 << 14, lots)
    priority = lots * amount + jnp.arange(amount)
    return lax.top_k(priority.astype(jnp.int32), top)[1].astype(jnp.int32)


def centred(rng, shape, spread, reach, split=(), held_as=jnp.bfloat16):
    values = jax.random.normal(rng, shape, jnp.float32) * spread
    if len(split) > 0:
        values = level_of(rng, shape, split, -0.22, 0.18) * values
    return jnp.clip(values, min=-reach, max=reach).astype(held_as)


def setup_inputs(seed: int = 0) -> dict:
    key_of = jax.random.split(jax.random.key(seed), 15)
    features = centred(key_of[0], (C, NX, NY, NZ), 1.0, 6.0, ((1, 8), (2, 4), (3, 8)))
    dest_bricks = different_ones(key_of[1], BLOCKS, GROUP, 1, 512)
    cell_ids = with_ends(jax.random.randint(key_of[2], (BLOCKS, PB), 0, CELLS), jax.random.fold_in(key_of[2], 1), 0, CELLS - 1).astype(jnp.int32)
    cic_masses = jnp.clip(0.25 + 3.75 * jax.random.uniform(key_of[3], (BLOCKS, PB), jnp.float32) ** level_of(key_of[3], (BLOCKS, PB), ((0, 256),), -0.2, 0.2), 0.25, 4.0).astype(jnp.bfloat16)
    live_counts = with_ends(jax.random.randint(key_of[4], (DEVICES,), NB // 4, NB + 1), jax.random.fold_in(key_of[4], 1), NB // 4, NB).astype(jnp.int32)
    style_vector = centred(key_of[5], (STYLE,), 1.0, 6.0, (), jnp.float32)
    affine_first = centred(key_of[6], (STYLE, C), STYLE ** -0.5, 0.25, (), jnp.float32)
    kernel_first = centred(key_of[7], (27, C, C), (27 * C) ** -0.5, 0.15625)
    bias_first = jnp.clip(jax.random.uniform(key_of[8], (C,), jnp.float32, -0.5, 0.5), -0.5, 0.5)
    gain_first = jnp.clip(jnp.exp(jax.random.uniform(key_of[9], (C,), jnp.float32, math.log(1.0), math.log(4.0))), 1.0, 4.0)
    affine_second = centred(key_of[10], (STYLE, C), STYLE ** -0.5, 0.25, (), jnp.float32)
    kernel_second = centred(key_of[11], (27, C, C), (27 * C) ** -0.5, 0.15625)
    bias_second = jnp.clip(jax.random.uniform(key_of[12], (C,), jnp.float32, -0.5, 0.5), -0.5, 0.5)
    gain_second = jnp.clip(jnp.exp(jax.random.uniform(key_of[13], (C,), jnp.float32, math.log(1.0), math.log(4.0))), 1.0, 4.0)
    return dict(features=features, dest_bricks=dest_bricks, cell_ids=cell_ids, cic_masses=cic_masses, live_counts=live_counts, style_vector=style_vector, affine_first=affine_first, kernel_first=kernel_first, bias_first=bias_first, gain_first=gain_first, affine_second=affine_second, kernel_second=kernel_second, bias_second=bias_second, gain_second=gain_second)


def modulate(kernel, style_vector, affine):
    styles = jnp.dot(style_vector[None, :], affine, precision=lax.Precision.HIGHEST, preferred_element_type=jnp.float32)[0] + 1.0
    scaled = kernel.astype(jnp.float32) * styles[None, None, :]
    demod = lax.rsqrt(lax.optimization_barrier(jnp.sum(scaled * scaled, axis=(0, 2))) + 1e-08)
    return (scaled * demod[None, :, None]).astype(jnp.bfloat16)

def activate(values):
    return jnp.where(values >= 0, values, 0.2 * values) * jnp.sqrt(jnp.float32(2.0))

def styled_layer(inputs, kernel, style_vector, affine, bias, gain, density):
    modulated = modulate(kernel, style_vector, affine).astype(jnp.float32)
    chans = modulated.shape[1]
    kernel_full = modulated.reshape(3, 3, 3, chans, chans).transpose(3, 4, 0, 1, 2)
    padded = jnp.pad(inputs.astype(jnp.float32), ((0, 0), (1, 1), (1, 1), (1, 1)), mode='wrap')
    convolved = lax.conv_general_dilated(padded[None], kernel_full, (1, 1, 1), 'VALID', dimension_numbers=('NCDHW', 'OIDHW', 'NCDHW'), precision=lax.Precision.HIGHEST)[0]
    summed = convolved + gain[:, None, None, None] * density[None] + bias[:, None, None, None]
    return activate(summed)

def reference(features, dest_bricks, cell_ids, cic_masses, live_counts, style_vector, affine_first, kernel_first, bias_first, gain_first, affine_second, kernel_second, bias_second, gain_second):
    block_index = jnp.arange(BLOCKS, dtype=jnp.int32)
    source = block_index // NB
    live = block_index % NB < live_counts[source]
    slab = source // GROUP
    brick = slab * GROUP + dest_bricks[:, 0]
    flat = (brick[:, None] * CELLS + cell_ids).reshape(-1).astype(jnp.int32)
    masses = (cic_masses.astype(jnp.float32) * live[:, None].astype(jnp.float32)).reshape(-1)
    painted = jax.ops.segment_sum(masses, flat, num_segments=DEVICES * CELLS)
    density = painted.reshape(N_GX, N_GY, N_GZ, BX, BY, BZ).transpose(0, 3, 1, 4, 2, 5).reshape(NX, NY, NZ)
    hidden = styled_layer(features, kernel_first, style_vector, affine_first, bias_first, gain_first, density).astype(jnp.bfloat16)
    result = styled_layer(hidden, kernel_second, style_vector, affine_second, bias_second, gain_second, density)
    return result.astype(jnp.bfloat16)
```

```python
import functools

import jax
import jax.numpy as jnp
from jax import lax
from jax.experimental import pallas as pl
from jax.experimental.pallas import tpu as pltpu
from jax.sharding import PartitionSpec as P

MESH = pl.DeviceIdType.MESH
F32 = jnp.float32
BF16 = jnp.bfloat16
NT = (((1,), (1,)), ((), ()))
SIDES = [(da, db, dc) for da in (0, -1, 1) for db in (0, -1, 1) for dc in (-1, 1)]
PLANAR = [(1, 0), (-1, 0), (0, 1), (0, -1), (1, 1), (1, -1), (-1, 1), (-1, -1)]


def shifted(sizes, me, move):
    return tuple((m + d + n) % n for m, d, n in zip(me, move, sizes))


def column(row):
    n = row.shape[1]
    eye = lax.broadcasted_iota(jnp.int32, (n, n), 0) == lax.broadcasted_iota(jnp.int32, (n, n), 1)
    return jnp.sum(jnp.where(eye, jnp.broadcast_to(row, (n, n)), 0.0), axis=1, keepdims=True)


def modulate(kernel_ref, style, affine_ref, main_ref, edge_ref):
    styles = (
        jnp.dot(style, affine_ref[...], precision=lax.Precision.HIGHEST, preferred_element_type=F32)
        + 1.0
    )
    total = jnp.zeros((64, 64), F32)
    for k in range(27):
        scaled = kernel_ref[k].astype(F32) * styles
        total = total + scaled * scaled
    demod = lax.rsqrt(jnp.sum(total, axis=1, keepdims=True) + 1e-08)

    def tap(k):
        return kernel_ref[k].astype(F32) * styles * demod

    zero = jnp.zeros((64, 64), F32)
    for g in range(3):
        for pair in range(5):
            left = tap(6 * pair + g)
            right = tap(6 * pair + 3 + g) if pair < 4 else zero
            main_ref[pl.ds(64 * g, 64), pl.ds(128 * pair, 128)] = jnp.concatenate(
                [left, right], axis=1
            ).astype(BF16)
    for ef in range(9):
        edge_ref[pl.ds(0, 64), pl.ds(128 * ef, 128)] = jnp.concatenate(
            [zero, tap(3 * ef)], axis=1
        ).astype(BF16)
        edge_ref[pl.ds(64, 64), pl.ds(128 * ef, 128)] = jnp.concatenate(
            [tap(3 * ef + 2), zero], axis=1
        ).astype(BF16)


def pack_edges(cells_ref, pick, edge_ref):
    rows = jnp.concatenate([cells_ref[1 + r // 8, 1 + r % 8] for r in range(16)], axis=1)
    both = lax.dot_general(pick, rows, NT, preferred_element_type=F32)
    edge_ref[...] = jnp.concatenate([both[:16], both[16:]], axis=1).astype(BF16)


def halo_copies(sizes, me, cells_ref, edge_ref, got_ref, sems):
    planar_send, planar_recv, edge_send, edge_recv = sems
    copies = []
    for n, (da, db) in enumerate(PLANAR):
        src_x = {1: pl.ds(2, 1), -1: pl.ds(1, 1), 0: pl.ds(1, 2)}[da]
        dst_x = {1: pl.ds(0, 1), -1: pl.ds(3, 1), 0: pl.ds(1, 2)}[da]
        src_y = {1: pl.ds(8, 1), -1: pl.ds(1, 1), 0: pl.ds(1, 8)}[db]
        dst_y = {1: pl.ds(0, 1), -1: pl.ds(9, 1), 0: pl.ds(1, 8)}[db]
        copies.append(
            pltpu.make_async_remote_copy(
                src_ref=cells_ref.at[src_x, src_y],
                dst_ref=cells_ref.at[dst_x, dst_y],
                send_sem=planar_send.at[n],
                recv_sem=planar_recv.at[n],
                device_id=shifted(sizes, me, (da, db, 0)),
                device_id_type=MESH,
            )
        )
    edges = [
        pltpu.make_async_remote_copy(
            src_ref=edge_ref,
            dst_ref=got_ref.at[n],
            send_sem=edge_send,
            recv_sem=edge_recv,
            device_id=shifted(sizes, me, move),
            device_id_type=MESH,
        )
        for n, move in enumerate(SIDES)
    ]
    return copies, edges


def wait_edges(got_ref, sem):
    pltpu.make_async_copy(got_ref, got_ref, sem).wait()


def unpack_edges(got_ref, ring_ref):
    lane = lax.broadcasted_iota(jnp.int32, (16, 128), 1)
    for da in (0, -1, 1):
        for db in (0, -1, 1):
            low = got_ref[SIDES.index((da, db, 1))].astype(F32)
            high = got_ref[SIDES.index((da, db, -1))].astype(F32)
            tile = jnp.where(lane < 64, high, low)
            for x in {0: (0, 1), 1: (1,), -1: (0,)}[da]:
                to_x = {0: 1 + x, 1: 0, -1: 3}[da]
                if db == 0:
                    ring_ref[to_x, pl.ds(1, 8)] = tile[8 * x : 8 * x + 8]
                elif db == 1:
                    ring_ref[to_x, pl.ds(0, 1)] = tile[8 * x + 7 : 8 * x + 8]
                else:
                    ring_ref[to_x, pl.ds(9, 1)] = tile[8 * x : 8 * x + 1]


def convolve(cells_ref, ring_ref, main_ref, edge_ref, emit):
    window = jnp.concatenate(
        [
            jnp.concatenate([ring_ref[e + x, pl.ds(f, 8)] for x in range(2)], axis=0)
            for e in range(3)
            for f in range(3)
        ],
        axis=1,
    ).astype(BF16)
    ends = lax.dot_general(edge_ref[...], window, NT, preferred_element_type=F32)
    lane = lax.broadcasted_iota(jnp.int32, (64, 128), 1)
    zero = jnp.zeros((64, 256), BF16)
    for pair in range(8):
        x, y = pair // 4, 2 * (pair % 4)
        stacked = jnp.concatenate(
            [
                jnp.concatenate([cells_ref[x + e, y + f], cells_ref[x + e, y + f + 1]], axis=1)
                for e in range(3)
                for f in range(3)
            ]
            + [zero],
            axis=0,
        )
        parts = jnp.dot(main_ref[...], stacked, preferred_element_type=F32)
        for half in range(2):
            row = 8 * x + y + half
            lanes = slice(128 * half, 128 * half + 128)
            low = jnp.where(
                lane == 0, ends[0:64, row : row + 1], pltpu.roll(parts[0:64, lanes], 1, 1)
            )
            high = jnp.where(
                lane == 127, ends[64:128, row : row + 1], pltpu.roll(parts[128:192, lanes], 127, 1)
            )
            emit(row, low + parts[64:128, lanes] + high)


def activate(values):
    return jnp.maximum(values, 0.2 * values) * jnp.sqrt(F32(2.0))


def paint(dest_ref, cell_ref, mass_ref, live_ref, left_ref, right_ref, part_ref):
    block = lax.broadcasted_iota(jnp.int32, (32, 64), 0)
    mass = jnp.where(block < live_ref[0], mass_ref[...].astype(F32), 0.0)
    key = dest_ref[...] * 2048 + cell_ref[...]
    key = jnp.concatenate([key[:16], key[16:]], axis=1)
    mass = jnp.concatenate([mass[:16], mass[16:]], axis=1)
    upper = key >> 7
    lower = key & 127
    tall = lax.broadcasted_iota(jnp.int32, (512, 128), 0)
    short = lax.broadcasted_iota(jnp.int32, (128, 128), 0)
    for n in range(16):
        lanes = pl.ds(128 * n, 128)
        left_ref[:, lanes] = jnp.where(
            tall == upper[n : n + 1], jnp.broadcast_to(mass[n : n + 1], (512, 128)), 0.0
        ).astype(BF16)
        right_ref[:, lanes] = jnp.where(short == lower[n : n + 1], 1.0, 0.0).astype(BF16)
    painted = lax.dot_general(left_ref[...], right_ref[...], NT, preferred_element_type=F32)
    part_ref[...] = painted.astype(BF16).reshape(32, 16, 128)


def body(
    sizes,
    features_ref,
    dest_ref,
    cell_ref,
    mass_ref,
    live_ref,
    style_ref,
    affine_first_ref,
    kernel_first_ref,
    bias_first_ref,
    gain_first_ref,
    affine_second_ref,
    kernel_second_ref,
    bias_second_ref,
    gain_second_ref,
    out_ref,
    left_ref,
    right_ref,
    part_ref,
    sums_ref,
    cells_first,
    cells_second,
    edge_first,
    edge_second,
    got_first,
    got_second,
    ring_ref,
    main_first,
    main_second,
    ends_first,
    ends_second,
    linear_ref,
    part_send,
    part_recv,
    planar_send,
    planar_recv,
    edge_send,
    edge_recv,
):
    n_gx, n_gy, n_gz = sizes
    slab = n_gy * n_gz
    me = (lax.axis_index("gx"), lax.axis_index("gy"), lax.axis_index("gz"))
    mine = me[1] * n_gz + me[2]

    def peer(j):
        other = (mine + j) % slab
        return other, (me[0], other // n_gz, other % n_gz)

    barrier = pltpu.get_barrier_semaphore()

    def greet(j, carry):
        pl.semaphore_signal(barrier, inc=1, device_id=peer(j)[1], device_id_type=MESH)
        return carry

    lax.fori_loop(1, slab, greet, 0)

    def greet_far(j, carry):
        move = (2 * (j // 9) - 1, (j // 3) % 3 - 1, j % 3 - 1)
        pl.semaphore_signal(
            barrier, inc=1, device_id=shifted(sizes, me, move), device_id_type=MESH
        )
        return carry

    lax.fori_loop(0, 18, greet_far, 0)

    for x in range(2):
        cells_first[1 + x, pl.ds(1, 8)] = features_ref[x]
    which = lax.broadcasted_iota(jnp.int32, (32, 2048), 0)
    place = lax.broadcasted_iota(jnp.int32, (32, 2048), 1)
    wanted = (which % 16) * 128 + (which // 16) * 127
    pick = jnp.where(place == wanted, 1.0, 0.0).astype(BF16)
    pack_edges(cells_first, pick, edge_first)
    paint(dest_ref, cell_ref, mass_ref, live_ref, left_ref, right_ref, part_ref)
    sums_ref[pl.ds(mine, 1)] = part_ref[pl.ds(mine, 1)]

    pl.semaphore_wait(barrier, slab - 1 + 18)

    def send_part(j, carry):
        other, device = peer(j)
        pltpu.make_async_remote_copy(
            src_ref=part_ref.at[other],
            dst_ref=sums_ref.at[mine],
            send_sem=part_send,
            recv_sem=part_recv,
            device_id=device,
            device_id_type=MESH,
        ).start()
        return carry

    lax.fori_loop(1, slab, send_part, 0)
    sems_first = (planar_send.at[0], planar_recv.at[0], edge_send.at[0], edge_recv.at[0])
    sems_second = (planar_send.at[1], planar_recv.at[1], edge_send.at[1], edge_recv.at[1])
    planar_one, edges_one = halo_copies(
        sizes, me, cells_first, edge_first, got_first, sems_first
    )
    for copy in planar_one + edges_one:
        copy.start()

    style = style_ref[...]
    modulate(kernel_first_ref, style, affine_first_ref, main_first, ends_first)
    modulate(kernel_second_ref, style, affine_second_ref, main_second, ends_second)
    bias_first = jnp.broadcast_to(column(bias_first_ref[...]), (64, 128))
    gain_first = jnp.broadcast_to(column(gain_first_ref[...]), (64, 128))
    bias_second = jnp.broadcast_to(column(bias_second_ref[...]), (64, 128))
    gain_second = jnp.broadcast_to(column(gain_second_ref[...]), (64, 128))

    for copy in planar_one:
        copy.wait()
    wait_edges(got_first, edge_recv.at[0])
    wait_edges(got_first, edge_send.at[0])
    unpack_edges(got_first, ring_ref)

    def keep(row, values):
        linear_ref[row] = values + bias_first

    convolve(cells_first, ring_ref, main_first, ends_first, keep)

    others = sums_ref.at[pl.ds(0, slab - 1)]
    pltpu.make_async_copy(others, others, part_recv).wait()
    pltpu.make_async_copy(others, others, part_send).wait()
    density = sums_ref[0].astype(F32)
    for n in range(1, slab):
        density = density + sums_ref[n].astype(F32)

    for row in range(16):
        values = linear_ref[row] + gain_first * density[row : row + 1]
        cells_second[1 + row // 8, 1 + row % 8] = activate(values).astype(BF16)
    pack_edges(cells_second, pick, edge_second)
    planar_two, edges_two = halo_copies(
        sizes, me, cells_second, edge_second, got_second, sems_second
    )
    for copy in planar_two + edges_two:
        copy.start()
    for copy in planar_two:
        copy.wait()
    wait_edges(got_second, edge_recv.at[1])
    wait_edges(got_second, edge_send.at[1])
    unpack_edges(got_second, ring_ref)

    def finish(row, values):
        out_ref[row // 8, row % 8] = activate(
            values + bias_second + gain_second * density[row : row + 1]
        ).astype(BF16)

    convolve(cells_second, ring_ref, main_second, ends_second, finish)


def shards(sizes, features, dest, cells, masses, live, style, *layers):
    slab = sizes[1] * sizes[2]
    affine_first, kernel_first, bias_first, gain_first = layers[:4]
    affine_second, kernel_second, bias_second, gain_second = layers[4:]
    vmem = pl.BlockSpec(memory_space=pltpu.VMEM)
    smem = pl.BlockSpec(memory_space=pltpu.SMEM)
    result = pl.pallas_call(
        functools.partial(body, sizes),
        out_shape=jax.ShapeDtypeStruct((2, 8, 64, 128), BF16),
        in_specs=[vmem] * 4 + [smem] + [vmem] * 9,
        out_specs=vmem,
        scratch_shapes=[
            pltpu.VMEM((512, 2048), BF16),
            pltpu.VMEM((128, 2048), BF16),
            pltpu.VMEM((slab, 16, 128), BF16),
            pltpu.VMEM((slab, 16, 128), BF16),
            pltpu.VMEM((4, 10, 64, 128), BF16),
            pltpu.VMEM((4, 10, 64, 128), BF16),
            pltpu.VMEM((16, 128), BF16),
            pltpu.VMEM((16, 128), BF16),
            pltpu.VMEM((18, 16, 128), BF16),
            pltpu.VMEM((18, 16, 128), BF16),
            pltpu.VMEM((4, 16, 128), F32),
            pltpu.VMEM((192, 640), BF16),
            pltpu.VMEM((192, 640), BF16),
            pltpu.VMEM((128, 1152), BF16),
            pltpu.VMEM((128, 1152), BF16),
            pltpu.VMEM((16, 64, 128), F32),
            pltpu.SemaphoreType.DMA,
            pltpu.SemaphoreType.DMA,
            pltpu.SemaphoreType.DMA((2, 8)),
            pltpu.SemaphoreType.DMA((2, 8)),
            pltpu.SemaphoreType.DMA((2,)),
            pltpu.SemaphoreType.DMA((2,)),
        ],
        compiler_params=pltpu.CompilerParams(
            collective_id=0, has_side_effects=True, vmem_limit_bytes=40 * 1024 * 1024
        ),
        name="styled_block",
    )(
        features.transpose(1, 2, 0, 3),
        dest,
        cells,
        masses,
        live,
        style.reshape(1, -1),
        affine_first,
        kernel_first,
        bias_first.reshape(1, -1),
        gain_first.reshape(1, -1),
        affine_second,
        kernel_second,
        bias_second.reshape(1, -1),
        gain_second.reshape(1, -1),
    )
    return result.transpose(2, 0, 1, 3)


def solution(mesh):
    sizes = (mesh.shape["gx"], mesh.shape["gy"], mesh.shape["gz"])
    spread = P(("gx", "gy", "gz"), None)
    return jax.shard_map(
        functools.partial(shards, sizes),
        mesh=mesh,
        in_specs=(P(None, "gx", "gy", "gz"), spread, spread, spread, P(("gx", "gy", "gz")))
        + (P(),) * 9,
        out_specs=P(None, "gx", "gy", "gz"),
        check_vma=False,
    )
```

```python
import functools

import jax
import jax.numpy as jnp
from jax import lax
from jax.experimental import pallas as pl
from jax.experimental.pallas import tpu as pltpu
from jax.sharding import PartitionSpec as P

MESH = pl.DeviceIdType.MESH
F32 = jnp.float32
BF16 = jnp.bfloat16
NT = (((1,), (1,)), ((), ()))
SIDES = [(da, db, dc) for da in (-1, 1, 0) for db in (-1, 1, 0) for dc in (-1, 1)]
PLANAR = [(1, 1), (1, -1), (-1, 1), (-1, -1), (0, 1), (0, -1), (1, 0), (-1, 0)]


def column(row):
    n = row.shape[1]
    eye = lax.broadcasted_iota(jnp.int32, (n, n), 0) == lax.broadcasted_iota(jnp.int32, (n, n), 1)
    return jnp.sum(jnp.where(eye, jnp.broadcast_to(row, (n, n)), 0.0), axis=1, keepdims=True)


def modulate(kernel_ref, style, affine, main_ref, edge_ref):
    styles = (
        lax.dot_general(
            style, affine, NT, precision=lax.Precision.HIGHEST, preferred_element_type=F32
        )
        + 1.0
    )
    total = jnp.zeros((64, 64), F32)
    for k in range(27):
        scaled = kernel_ref[k].astype(F32) * styles
        total = total + scaled * scaled
    demod = lax.rsqrt(jnp.sum(total, axis=1, keepdims=True) + 1e-08)

    def tap(k):
        return kernel_ref[k].astype(F32) * styles * demod

    zero = jnp.zeros((64, 64), F32)
    for g in range(3):
        for e in range(3):
            for half in range(2):
                k = 9 * e + 6 * half + g
                right = zero if half else tap(k + 3)
                main_ref[pl.ds(64 * g, 64), pl.ds(256 * e + 128 * half, 128)] = jnp.concatenate(
                    [tap(k), right], axis=1
                ).astype(BF16)
    for ef in range(9):
        edge_ref[pl.ds(0, 64), pl.ds(128 * ef, 128)] = jnp.concatenate(
            [zero, tap(3 * ef)], axis=1
        ).astype(BF16)
        edge_ref[pl.ds(64, 64), pl.ds(128 * ef, 128)] = jnp.concatenate(
            [tap(3 * ef + 2), zero], axis=1
        ).astype(BF16)


def pack_edges(cells_ref, pick, edge_ref):
    rows = jnp.concatenate([cells_ref[1 + r // 8, 1 + r % 8] for r in range(16)], axis=1)
    both = lax.dot_general(pick, rows, NT, preferred_element_type=F32)
    edge_ref[...] = jnp.concatenate([both[:16], both[16:]], axis=1).astype(BF16)


def unpack_edges(got_ref, ring_ref):
    lane = lax.broadcasted_iota(jnp.int32, (16, 128), 1)
    for da in (0, -1, 1):
        for db in (0, -1, 1):
            low = got_ref[SIDES.index((da, db, 1))].astype(F32)
            high = got_ref[SIDES.index((da, db, -1))].astype(F32)
            tile = jnp.where(lane < 64, high, low)
            for x in {0: (0, 1), 1: (1,), -1: (0,)}[da]:
                to_x = {0: 1 + x, 1: 0, -1: 3}[da]
                if db == 0:
                    ring_ref[to_x, pl.ds(1, 8)] = tile[8 * x : 8 * x + 8]
                elif db == 1:
                    ring_ref[to_x, pl.ds(0, 1)] = tile[8 * x + 7 : 8 * x + 8]
                else:
                    ring_ref[to_x, pl.ds(9, 1)] = tile[8 * x : 8 * x + 1]


def stack(cells_ref, plane, y):
    zero = jnp.zeros((64, 256), BF16)
    return jnp.concatenate(
        [
            jnp.concatenate([cells_ref[plane, y + f], cells_ref[plane, y + f + 1]], axis=1)
            for f in range(3)
        ]
        + [zero],
        axis=0,
    )


def taps(main_ref, e, stacked):
    return jnp.dot(main_ref[:, pl.ds(256 * e, 256)], stacked, preferred_element_type=F32)


def convolve_own(cells_ref, main_ref, parts_ref):
    for pair in range(4):
        near = stack(cells_ref, 1, 2 * pair)
        far = stack(cells_ref, 2, 2 * pair)
        parts_ref[pair] = taps(main_ref, 1, near) + taps(main_ref, 2, far)
        parts_ref[4 + pair] = taps(main_ref, 0, near) + taps(main_ref, 1, far)


def convolve_halo(cells_ref, ring_ref, main_ref, edge_ref, parts_ref, emit):
    window = jnp.concatenate(
        [
            jnp.concatenate([ring_ref[e + x, pl.ds(f, 8)] for x in range(2)], axis=0)
            for e in range(3)
            for f in range(3)
        ],
        axis=1,
    ).astype(BF16)
    ends = lax.dot_general(edge_ref[...], window, NT, preferred_element_type=F32)
    lane = lax.broadcasted_iota(jnp.int32, (64, 128), 1)
    for pair in range(8):
        x, y = pair // 4, 2 * (pair % 4)
        parts = parts_ref[pair] + taps(main_ref, 2 * x, stack(cells_ref, 3 * x, y))
        for half in range(2):
            row = 8 * x + y + half
            lanes = slice(128 * half, 128 * half + 128)
            low = jnp.where(
                lane == 0, ends[0:64, row : row + 1], pltpu.roll(parts[0:64, lanes], 1, 1)
            )
            high = jnp.where(
                lane == 127, ends[64:128, row : row + 1], pltpu.roll(parts[128:192, lanes], 127, 1)
            )
            emit(row, low + parts[64:128, lanes] + high)


def activate(values):
    return jnp.maximum(values, 0.2 * values) * jnp.sqrt(F32(2.0))


def paint(dest, cells, mass, live, left_ref, right_ref, part_ref):
    block = lax.broadcasted_iota(jnp.int32, (32, 64), 0)
    mass = jnp.where(block < jnp.broadcast_to(live, (32, 64)), mass.astype(F32), 0.0)
    n = dest.shape[1]
    eye = lax.broadcasted_iota(jnp.int32, (n, n), 0) == lax.broadcasted_iota(jnp.int32, (n, n), 1)
    spread = jnp.where(eye, jnp.broadcast_to(dest.astype(F32), (n, n)), 0.0)
    base = jnp.sum(spread, axis=1, keepdims=True).astype(jnp.int32)
    key = base * 2048 + cells
    key = jnp.concatenate([key[:16], key[16:]], axis=1)
    mass = jnp.concatenate([mass[:16], mass[16:]], axis=1)
    upper = key >> 7
    lower = key & 127
    tall = lax.broadcasted_iota(jnp.int32, (512, 128), 0)
    short = lax.broadcasted_iota(jnp.int32, (128, 128), 0)
    for n in range(16):
        lanes = pl.ds(128 * n, 128)
        left_ref[:, lanes] = jnp.where(
            tall == upper[n : n + 1], jnp.broadcast_to(mass[n : n + 1], (512, 128)), 0.0
        ).astype(BF16)
        right_ref[:, lanes] = jnp.where(short == lower[n : n + 1], 1.0, 0.0).astype(BF16)
    painted = lax.dot_general(left_ref[...], right_ref[...], NT, preferred_element_type=F32)
    part_ref[...] = painted.astype(BF16).reshape(32, 16, 128)


def body(sizes, n_in, *refs):
    sources = refs[:n_in]
    out_ref = refs[n_in]
    held = refs[n_in + 1 : 2 * n_in + 1]
    (
        left_ref,
        right_ref,
        part_ref,
        sums_ref,
        cells_first,
        cells_second,
        edge_first,
        edge_second,
        got_first,
        got_second,
        ring_ref,
        main_first,
        main_second,
        ends_first,
        ends_second,
        parts_ref,
        fetch_sem,
        part_sem,
        halo_sem,
        edge_sem,
    ) = refs[2 * n_in + 1 :]
    n_gx, n_gy, n_gz = sizes
    slab = n_gy * n_gz
    me = (lax.axis_index("gx"), lax.axis_index("gy"), lax.axis_index("gz"))
    mine = me[1] * n_gz + me[2]
    at_x = {d: (me[0] + d + n_gx) % n_gx for d in (-1, 0, 1)}
    at_y = [(me[1] + d) % n_gy for d in range(n_gy)]
    at_z = [(me[2] + d) % n_gz for d in range(n_gz)]

    def place(move):
        return (at_x[move[0]], at_y[move[1] % n_gy], at_z[move[2] % n_gz])

    others = [(dy, dz) for dy in range(n_gy) for dz in range(n_gz) if (dy, dz) != (0, 0)]

    fetches = [
        pltpu.make_async_copy(source, kept, fetch_sem.at[n])
        for n, (source, kept) in enumerate(zip(sources, held))
    ]
    for fetch in fetches[:5]:
        fetch.start()
    barrier = pltpu.get_barrier_semaphore()
    for dy, dz in others:
        pl.semaphore_signal(
            barrier, inc=1, device_id=(me[0], at_y[dy], at_z[dz]), device_id_type=MESH
        )
    for da in (-1, 1):
        for db in (-1, 0, 1):
            for dc in (-1, 0, 1):
                pl.semaphore_signal(
                    barrier, inc=1, device_id=place((da, db, dc)), device_id_type=MESH
                )
    for fetch in fetches[5:]:
        fetch.start()

    dest, cells, mass, live, features, style, *layers = held
    for fetch in fetches[:4]:
        fetch.wait()
    paint(dest[...], cells[...], mass[...], live[...].reshape(1, 1), left_ref, right_ref, part_ref)
    sums_ref[pl.ds(mine, 1)] = part_ref[pl.ds(mine, 1)]

    which = lax.broadcasted_iota(jnp.int32, (32, 2048), 0)
    spot = lax.broadcasted_iota(jnp.int32, (32, 2048), 1)
    wanted = (which % 16) * 128 + (which // 16) * 127
    pick = jnp.where(spot == wanted, 1.0, 0.0).astype(BF16)

    fetches[4].wait()
    for x in range(2):
        turned = jnp.transpose(features[:, x].astype(F32), (1, 0, 2))
        cells_first[1 + x, pl.ds(1, 8)] = turned.astype(BF16)
    pack_edges(cells_first, pick, edge_first)

    pl.semaphore_wait(barrier, slab - 1 + 18)

    for dy, dz in others:
        pltpu.make_async_remote_copy(
            src_ref=part_ref.at[at_y[dy] * n_gz + at_z[dz]],
            dst_ref=sums_ref.at[mine],
            send_sem=part_sem.at[0],
            recv_sem=part_sem.at[1],
            device_id=(me[0], at_y[dy], at_z[dz]),
            device_id_type=MESH,
        ).start()

    def start_halo(layer, cells_ref, edge_ref, got_ref):
        for n, move in enumerate(SIDES):
            pltpu.make_async_remote_copy(
                src_ref=edge_ref,
                dst_ref=got_ref.at[n],
                send_sem=edge_sem.at[layer, 0],
                recv_sem=edge_sem.at[layer, 1],
                device_id=place(move),
                device_id_type=MESH,
            ).start()
        for da, db in PLANAR:
            group = 0 if da == 0 else 2
            src_x = {1: pl.ds(2, 1), -1: pl.ds(1, 1), 0: pl.ds(1, 2)}[da]
            dst_x = {1: pl.ds(0, 1), -1: pl.ds(3, 1), 0: pl.ds(1, 2)}[da]
            src_y = {1: pl.ds(8, 1), -1: pl.ds(1, 1), 0: pl.ds(1, 8)}[db]
            dst_y = {1: pl.ds(0, 1), -1: pl.ds(9, 1), 0: pl.ds(1, 8)}[db]
            pltpu.make_async_remote_copy(
                src_ref=cells_ref.at[src_x, src_y],
                dst_ref=cells_ref.at[dst_x, dst_y],
                send_sem=halo_sem.at[layer, group],
                recv_sem=halo_sem.at[layer, group + 1],
                device_id=place((da, db, 0)),
                device_id_type=MESH,
            ).start()

    def wait_for(ref, sem):
        pltpu.make_async_copy(ref, ref, sem).wait()

    def wait_beside(layer, cells_ref):
        four = cells_ref.at[pl.ds(0, 1), pl.ds(0, 4)]
        for sem in range(2):
            wait_for(four, halo_sem.at[layer, sem])

    def wait_across(layer, cells_ref, got_ref):
        twenty = cells_ref.at[pl.ds(0, 2), pl.ds(0, 10)]
        for sem in range(2):
            wait_for(twenty, halo_sem.at[layer, 2 + sem])
            wait_for(got_ref, edge_sem.at[layer, sem])

    start_halo(0, cells_first, edge_first, got_first)

    for fetch in fetches[5:]:
        fetch.wait()
    style = style[...]
    modulate(layers[1], style, layers[0][...], main_first, ends_first)
    modulate(layers[5], style, layers[4][...], main_second, ends_second)
    bias_first, gain_first, bias_second, gain_second = (
        jnp.broadcast_to(column(layers[n][...]), (64, 128)) for n in (2, 3, 6, 7)
    )

    wait_beside(0, cells_first)
    convolve_own(cells_first, main_first, parts_ref)
    rest = sums_ref.at[pl.ds(0, slab - 1)]
    wait_for(rest, part_sem.at[1])
    wait_for(rest, part_sem.at[0])
    density = sums_ref[0].astype(F32)
    for n in range(1, slab):
        density = density + sums_ref[n].astype(F32)
    wait_across(0, cells_first, got_first)
    unpack_edges(got_first, ring_ref)

    def keep(row, values):
        cells_second[1 + row // 8, 1 + row % 8] = activate(
            values + gain_first * density[row : row + 1] + bias_first
        ).astype(BF16)

    convolve_halo(cells_first, ring_ref, main_first, ends_first, parts_ref, keep)
    pack_edges(cells_second, pick, edge_second)
    start_halo(1, cells_second, edge_second, got_second)
    wait_beside(1, cells_second)
    convolve_own(cells_second, main_second, parts_ref)
    wait_across(1, cells_second, got_second)
    unpack_edges(got_second, ring_ref)

    def finish(row, values):
        out_ref[row // 8, row % 8] = activate(
            values + gain_second * density[row : row + 1] + bias_second
        ).astype(BF16)

    convolve_halo(cells_second, ring_ref, main_second, ends_second, parts_ref, finish)


def shards(sizes, features, dest, cells, masses, live, style, *layers):
    slab = sizes[1] * sizes[2]
    operands = [
        dest.reshape(1, -1),
        cells,
        masses,
        live,
        features,
        style.reshape(1, -1),
    ]
    for affine, kernel, bias, gain in (layers[:4], layers[4:]):
        operands += [affine.T, kernel, bias.reshape(1, -1), gain.reshape(1, -1)]
    result = pl.pallas_call(
        functools.partial(body, sizes, len(operands)),
        out_shape=jax.ShapeDtypeStruct((2, 8, 64, 128), BF16),
        in_specs=[pl.BlockSpec(memory_space=pltpu.HBM)] * len(operands),
        out_specs=pl.BlockSpec(memory_space=pltpu.VMEM),
        scratch_shapes=[pltpu.VMEM(x.shape, x.dtype) for x in operands]
        + [
            pltpu.VMEM((512, 2048), BF16),
            pltpu.VMEM((128, 2048), BF16),
            pltpu.VMEM((slab, 16, 128), BF16),
            pltpu.VMEM((slab, 16, 128), BF16),
            pltpu.VMEM((4, 10, 64, 128), BF16),
            pltpu.VMEM((4, 10, 64, 128), BF16),
            pltpu.VMEM((16, 128), BF16),
            pltpu.VMEM((16, 128), BF16),
            pltpu.VMEM((18, 16, 128), BF16),
            pltpu.VMEM((18, 16, 128), BF16),
            pltpu.VMEM((4, 16, 128), F32),
            pltpu.VMEM((192, 768), BF16),
            pltpu.VMEM((192, 768), BF16),
            pltpu.VMEM((128, 1152), BF16),
            pltpu.VMEM((128, 1152), BF16),
            pltpu.VMEM((8, 192, 256), F32),
            pltpu.SemaphoreType.DMA((len(operands),)),
            pltpu.SemaphoreType.DMA((2,)),
            pltpu.SemaphoreType.DMA((2, 4)),
            pltpu.SemaphoreType.DMA((2, 2)),
        ],
        compiler_params=pltpu.CompilerParams(
            collective_id=0, has_side_effects=True, vmem_limit_bytes=63 * 1024 * 1024
        ),
        name="styled_block",
    )(*operands)
    return result.transpose(2, 0, 1, 3)


def solution(mesh):
    sizes = (mesh.shape["gx"], mesh.shape["gy"], mesh.shape["gz"])
    spread = P(("gx", "gy", "gz"), None)
    return jax.shard_map(
        functools.partial(shards, sizes),
        mesh=mesh,
        in_specs=(P(None, "gx", "gy", "gz"), spread, spread, spread, P(("gx", "gy", "gz")))
        + (P(),) * 9,
        out_specs=P(None, "gx", "gy", "gz"),
        check_vma=False,
    )
```

```python
import functools

import jax
import jax.numpy as jnp
from jax import lax
from jax.experimental import pallas as pl
from jax.experimental.pallas import tpu as pltpu
from jax.sharding import PartitionSpec as P

MESH = pl.DeviceIdType.MESH
F32 = jnp.float32
BF16 = jnp.bfloat16
NT = (((1,), (1,)), ((), ()))
SIDES = [(da, db, dc) for da in (-1, 1, 0) for db in (-1, 1, 0) for dc in (-1, 1)]
PLANAR = [(1, 1), (1, -1), (-1, 1), (-1, -1), (0, 1), (0, -1), (1, 0), (-1, 0)]


def column(row):
    n = row.shape[1]
    eye = lax.broadcasted_iota(jnp.int32, (n, n), 0) == lax.broadcasted_iota(jnp.int32, (n, n), 1)
    return jnp.sum(jnp.where(eye, jnp.broadcast_to(row, (n, n)), 0.0), axis=1, keepdims=True)


def modulate(kernel_ref, style, affine, main_ref, edge_ref):
    styles = (
        lax.dot_general(
            style, affine, NT, precision=lax.Precision.HIGHEST, preferred_element_type=F32
        )
        + 1.0
    )
    total = jnp.zeros((64, 64), F32)
    for k in range(27):
        scaled = kernel_ref[k].astype(F32) * styles
        total = total + scaled * scaled
    demod = lax.rsqrt(jnp.sum(total, axis=1, keepdims=True) + 1e-08)

    def tap(k):
        return kernel_ref[k].astype(F32) * styles * demod

    zero = jnp.zeros((64, 64), F32)
    for g in range(3):
        for e in range(3):
            for half in range(2):
                k = 9 * e + 6 * half + g
                right = zero if half else tap(k + 3)
                main_ref[pl.ds(64 * g, 64), pl.ds(256 * e + 128 * half, 128)] = jnp.concatenate(
                    [tap(k), right], axis=1
                ).astype(BF16)
    for ef in range(9):
        edge_ref[pl.ds(0, 64), pl.ds(128 * ef, 128)] = jnp.concatenate(
            [zero, tap(3 * ef)], axis=1
        ).astype(BF16)
        edge_ref[pl.ds(64, 64), pl.ds(128 * ef, 128)] = jnp.concatenate(
            [tap(3 * ef + 2), zero], axis=1
        ).astype(BF16)


def pack_edges(cells_ref, pick, edge_ref):
    rows = jnp.concatenate([cells_ref[1 + r // 8, 1 + r % 8] for r in range(16)], axis=1)
    both = lax.dot_general(pick, rows, NT, preferred_element_type=F32)
    edge_ref[...] = jnp.concatenate([both[:16], both[16:]], axis=1).astype(BF16)


def unpack_edges(got_ref, ring_ref):
    lane = lax.broadcasted_iota(jnp.int32, (16, 128), 1)
    for da in (0, -1, 1):
        for db in (0, -1, 1):
            low = got_ref[SIDES.index((da, db, 1))].astype(F32)
            high = got_ref[SIDES.index((da, db, -1))].astype(F32)
            tile = jnp.where(lane < 64, high, low)
            for x in {0: (0, 1), 1: (1,), -1: (0,)}[da]:
                to_x = {0: 1 + x, 1: 0, -1: 3}[da]
                if db == 0:
                    ring_ref[to_x, pl.ds(1, 8)] = tile[8 * x : 8 * x + 8]
                elif db == 1:
                    ring_ref[to_x, pl.ds(0, 1)] = tile[8 * x + 7 : 8 * x + 8]
                else:
                    ring_ref[to_x, pl.ds(9, 1)] = tile[8 * x : 8 * x + 1]


def stack(cells_ref, plane, y):
    zero = jnp.zeros((64, 256), BF16)
    return jnp.concatenate(
        [
            jnp.concatenate([cells_ref[plane, y + f], cells_ref[plane, y + f + 1]], axis=1)
            for f in range(3)
        ]
        + [zero],
        axis=0,
    )


def taps(main_ref, e, stacked):
    return jnp.dot(main_ref[:, pl.ds(256 * e, 256)], stacked, preferred_element_type=F32)


def convolve_own(cells_ref, main_ref, parts_ref):
    for pair in range(4):
        near = stack(cells_ref, 1, 2 * pair)
        far = stack(cells_ref, 2, 2 * pair)
        parts_ref[pair] = taps(main_ref, 1, near) + taps(main_ref, 2, far)
        parts_ref[4 + pair] = taps(main_ref, 0, near) + taps(main_ref, 1, far)


def convolve_ends(ring_ref, edge_ref):
    window = jnp.concatenate(
        [
            jnp.concatenate([ring_ref[e + x, pl.ds(f, 8)] for x in range(2)], axis=0)
            for e in range(3)
            for f in range(3)
        ],
        axis=1,
    ).astype(BF16)
    return lax.dot_general(edge_ref[...], window, NT, preferred_element_type=F32)


def convolve_halo(cells_ref, ends, main_ref, parts_ref, emit):
    lane = lax.broadcasted_iota(jnp.int32, (64, 128), 1)
    for pair in range(8):
        x, y = pair // 4, 2 * (pair % 4)
        parts = parts_ref[pair] + taps(main_ref, 2 * x, stack(cells_ref, 3 * x, y))
        for half in range(2):
            row = 8 * x + y + half
            lanes = slice(128 * half, 128 * half + 128)
            low = jnp.where(
                lane == 0, ends[0:64, row : row + 1], pltpu.roll(parts[0:64, lanes], 1, 1)
            )
            high = jnp.where(
                lane == 127, ends[64:128, row : row + 1], pltpu.roll(parts[128:192, lanes], 127, 1)
            )
            emit(row, low + parts[64:128, lanes] + high)


def activate(values):
    return jnp.maximum(values, 0.2 * values) * jnp.sqrt(F32(2.0))


def paint(dest, cells, mass, live, left_ref, right_ref, part_ref):
    block = lax.broadcasted_iota(jnp.int32, (32, 64), 0)
    mass = jnp.where(block < live, mass.astype(F32), 0.0)
    n = dest.shape[1]
    eye = lax.broadcasted_iota(jnp.int32, (n, n), 0) == lax.broadcasted_iota(jnp.int32, (n, n), 1)
    spread = jnp.where(eye, jnp.broadcast_to(dest.astype(F32), (n, n)), 0.0)
    base = jnp.sum(spread, axis=1, keepdims=True).astype(jnp.int32)
    key = base * 2048 + cells
    key = jnp.concatenate([key[:16], key[16:]], axis=1)
    mass = jnp.concatenate([mass[:16], mass[16:]], axis=1)
    upper = key >> 7
    lower = key & 127
    tall = lax.broadcasted_iota(jnp.int32, (512, 128), 0)
    short = lax.broadcasted_iota(jnp.int32, (128, 128), 0)
    for n in range(16):
        lanes = pl.ds(128 * n, 128)
        left_ref[:, lanes] = jnp.where(
            tall == upper[n : n + 1], jnp.broadcast_to(mass[n : n + 1], (512, 128)), 0.0
        ).astype(BF16)
        right_ref[:, lanes] = jnp.where(short == lower[n : n + 1], 1.0, 0.0).astype(BF16)
    painted = lax.dot_general(left_ref[...], right_ref[...], NT, preferred_element_type=F32)
    part_ref[...] = painted.astype(BF16).reshape(32, 16, 128)


def body(sizes, n_in, live_ref, *refs):
    sources = refs[:n_in]
    out_ref = refs[n_in]
    held = refs[n_in + 1 : 2 * n_in + 1]
    (
        left_ref,
        right_ref,
        part_ref,
        sums_ref,
        cells_first,
        cells_second,
        edge_first,
        edge_second,
        got_first,
        got_second,
        ring_ref,
        main_first,
        main_second,
        ends_first,
        ends_second,
        parts_ref,
        fetch_sem,
        part_sem,
        halo_sem,
        edge_sem,
    ) = refs[2 * n_in + 1 :]
    n_gx, n_gy, n_gz = sizes
    slab = n_gy * n_gz
    me = (lax.axis_index("gx"), lax.axis_index("gy"), lax.axis_index("gz"))
    mine = me[1] * n_gz + me[2]
    at_x = {d: (me[0] + d + n_gx) % n_gx for d in (-1, 0, 1)}
    at_y = [(me[1] + d) % n_gy for d in range(n_gy)]
    at_z = [(me[2] + d) % n_gz for d in range(n_gz)]

    def place(move):
        return (at_x[move[0]], at_y[move[1] % n_gy], at_z[move[2] % n_gz])

    others = [(dy, dz) for dy in range(n_gy) for dz in range(n_gz) if (dy, dz) != (0, 0)]

    fetches = [
        pltpu.make_async_copy(source, kept, fetch_sem.at[n])
        for n, (source, kept) in enumerate(zip(sources, held))
    ]
    for fetch in fetches[:4]:
        fetch.start()
    barrier = pltpu.get_barrier_semaphore()
    for dy, dz in others:
        pl.semaphore_signal(
            barrier, inc=1, device_id=(me[0], at_y[dy], at_z[dz]), device_id_type=MESH
        )
    for da in (-1, 1):
        for db in (-1, 0, 1):
            for dc in (-1, 0, 1):
                pl.semaphore_signal(
                    barrier, inc=1, device_id=place((da, db, dc)), device_id_type=MESH
                )
    for fetch in fetches[4:]:
        fetch.start()

    features, dest, cells, mass, style, *layers = held
    which = lax.broadcasted_iota(jnp.int32, (32, 2048), 0)
    spot = lax.broadcasted_iota(jnp.int32, (32, 2048), 1)
    wanted = (which % 16) * 128 + (which // 16) * 127
    pick = jnp.where(spot == wanted, 1.0, 0.0).astype(BF16)

    fetches[0].wait()
    for x in range(2):
        turned = jnp.transpose(features[:, x].astype(F32), (1, 0, 2))
        cells_first[1 + x, pl.ds(1, 8)] = turned.astype(BF16)
    pack_edges(cells_first, pick, edge_first)

    pl.semaphore_wait(barrier, slab - 1 + 18)

    def start_halo(layer, cells_ref, edge_ref, got_ref):
        for n, move in enumerate(SIDES):
            pltpu.make_async_remote_copy(
                src_ref=edge_ref,
                dst_ref=got_ref.at[n],
                send_sem=edge_sem.at[layer, 0],
                recv_sem=edge_sem.at[layer, 1],
                device_id=place(move),
                device_id_type=MESH,
            ).start()
        for da, db in PLANAR:
            group = 0 if da == 0 else 2
            src_x = {1: pl.ds(2, 1), -1: pl.ds(1, 1), 0: pl.ds(1, 2)}[da]
            dst_x = {1: pl.ds(0, 1), -1: pl.ds(3, 1), 0: pl.ds(1, 2)}[da]
            src_y = {1: pl.ds(8, 1), -1: pl.ds(1, 1), 0: pl.ds(1, 8)}[db]
            dst_y = {1: pl.ds(0, 1), -1: pl.ds(9, 1), 0: pl.ds(1, 8)}[db]
            pltpu.make_async_remote_copy(
                src_ref=cells_ref.at[src_x, src_y],
                dst_ref=cells_ref.at[dst_x, dst_y],
                send_sem=halo_sem.at[layer, group],
                recv_sem=halo_sem.at[layer, group + 1],
                device_id=place((da, db, 0)),
                device_id_type=MESH,
            ).start()

    def wait_for(ref, sem):
        pltpu.make_async_copy(ref, ref, sem).wait()

    def wait_beside(layer, cells_ref):
        four = cells_ref.at[pl.ds(0, 1), pl.ds(0, 4)]
        for sem in range(2):
            wait_for(four, halo_sem.at[layer, sem])

    def wait_across(layer, cells_ref):
        twenty = cells_ref.at[pl.ds(0, 2), pl.ds(0, 10)]
        for sem in range(2):
            wait_for(twenty, halo_sem.at[layer, 2 + sem])

    def wait_edges(layer, got_ref):
        for sem in range(2):
            wait_for(got_ref, edge_sem.at[layer, sem])

    start_halo(0, cells_first, edge_first, got_first)
    for fetch in fetches[1:4]:
        fetch.wait()
    paint(dest[...], cells[...], mass[...], live_ref[0], left_ref, right_ref, part_ref)
    sums_ref[pl.ds(mine, 1)] = part_ref[pl.ds(mine, 1)]
    for dy, dz in others:
        pltpu.make_async_remote_copy(
            src_ref=part_ref.at[at_y[dy] * n_gz + at_z[dz]],
            dst_ref=sums_ref.at[mine],
            send_sem=part_sem.at[0],
            recv_sem=part_sem.at[1],
            device_id=(me[0], at_y[dy], at_z[dz]),
            device_id_type=MESH,
        ).start()


    for fetch in fetches[4:]:
        fetch.wait()
    style = style[...]
    modulate(layers[1], style, layers[0][...], main_first, ends_first)
    modulate(layers[5], style, layers[4][...], main_second, ends_second)
    bias_first, gain_first, bias_second, gain_second = (
        jnp.broadcast_to(column(layers[n][...]), (64, 128)) for n in (2, 3, 6, 7)
    )

    wait_beside(0, cells_first)
    convolve_own(cells_first, main_first, parts_ref)
    wait_edges(0, got_first)
    unpack_edges(got_first, ring_ref)
    ends = convolve_ends(ring_ref, ends_first)
    rest = sums_ref.at[pl.ds(0, slab - 1)]
    wait_for(rest, part_sem.at[1])
    wait_for(rest, part_sem.at[0])
    density = sums_ref[0].astype(F32)
    for n in range(1, slab):
        density = density + sums_ref[n].astype(F32)
    wait_across(0, cells_first)

    def keep(row, values):
        cells_second[1 + row // 8, 1 + row % 8] = activate(
            values + gain_first * density[row : row + 1] + bias_first
        ).astype(BF16)

    convolve_halo(cells_first, ends, main_first, parts_ref, keep)
    pack_edges(cells_second, pick, edge_second)
    start_halo(1, cells_second, edge_second, got_second)
    wait_beside(1, cells_second)
    convolve_own(cells_second, main_second, parts_ref)
    wait_edges(1, got_second)
    unpack_edges(got_second, ring_ref)
    ends_now = convolve_ends(ring_ref, ends_second)
    wait_across(1, cells_second)

    def finish(row, values):
        out_ref[row // 8, row % 8] = activate(
            values + gain_second * density[row : row + 1] + bias_second
        ).astype(BF16)

    convolve_halo(cells_second, ends_now, main_second, parts_ref, finish)


def shards(sizes, features, dest, cells, masses, live, style, *layers):
    slab = sizes[1] * sizes[2]
    operands = [
        features,
        dest.reshape(1, -1),
        cells,
        masses,
        style.reshape(1, -1),
    ]
    for affine, kernel, bias, gain in (layers[:4], layers[4:]):
        operands += [affine.T, kernel, bias.reshape(1, -1), gain.reshape(1, -1)]
    operands = [pltpu.with_memory_space_constraint(x, pltpu.HBM) for x in operands]
    result = pl.pallas_call(
        functools.partial(body, sizes, len(operands)),
        out_shape=pltpu.VMEM((2, 8, 64, 128), BF16),
        in_specs=[pl.BlockSpec(memory_space=pltpu.SMEM)]
        + [pl.BlockSpec(memory_space=pltpu.HBM)] * len(operands),
        out_specs=pl.BlockSpec(memory_space=pltpu.VMEM),
        scratch_shapes=[pltpu.VMEM(x.shape, x.dtype) for x in operands]
        + [
            pltpu.VMEM((512, 2048), BF16),
            pltpu.VMEM((128, 2048), BF16),
            pltpu.VMEM((slab, 16, 128), BF16),
            pltpu.VMEM((slab, 16, 128), BF16),
            pltpu.VMEM((4, 10, 64, 128), BF16),
            pltpu.VMEM((4, 10, 64, 128), BF16),
            pltpu.VMEM((16, 128), BF16),
            pltpu.VMEM((16, 128), BF16),
            pltpu.VMEM((18, 16, 128), BF16),
            pltpu.VMEM((18, 16, 128), BF16),
            pltpu.VMEM((4, 16, 128), F32),
            pltpu.VMEM((192, 768), BF16),
            pltpu.VMEM((192, 768), BF16),
            pltpu.VMEM((128, 1152), BF16),
            pltpu.VMEM((128, 1152), BF16),
            pltpu.VMEM((8, 192, 256), F32),
            pltpu.SemaphoreType.DMA((len(operands),)),
            pltpu.SemaphoreType.DMA((2,)),
            pltpu.SemaphoreType.DMA((2, 4)),
            pltpu.SemaphoreType.DMA((2, 2)),
        ],
        compiler_params=pltpu.CompilerParams(
            collective_id=0, has_side_effects=True, vmem_limit_bytes=40 * 1024 * 1024
        ),
        name="styled_block",
    )(live, *operands)
    return result.transpose(2, 0, 1, 3)


def solution(mesh):
    sizes = (mesh.shape["gx"], mesh.shape["gy"], mesh.shape["gz"])
    spread = P(("gx", "gy", "gz"), None)
    return jax.shard_map(
        functools.partial(shards, sizes),
        mesh=mesh,
        in_specs=(P(None, "gx", "gy", "gz"), spread, spread, spread, P(("gx", "gy", "gz")))
        + (P(),) * 9,
        out_specs=P(None, "gx", "gy", "gz"),
        check_vma=False,
    )
```

```python
import functools

import jax
import jax.numpy as jnp
from jax import lax
from jax.experimental import pallas as pl
from jax.experimental.pallas import tpu as pltpu
from jax.sharding import PartitionSpec as P

MESH = pl.DeviceIdType.MESH
F32 = jnp.float32
BF16 = jnp.bfloat16
NT = (((1,), (1,)), ((), ()))
SIDES = [(da, db, dc) for da in (-1, 1, 0) for db in (-1, 1, 0) for dc in (-1, 1)]
PLANAR = [(1, 1), (1, -1), (-1, 1), (-1, -1), (0, 1), (0, -1), (1, 0), (-1, 0)]


def column(row):
    n = row.shape[1]
    eye = lax.broadcasted_iota(jnp.int32, (n, n), 0) == lax.broadcasted_iota(jnp.int32, (n, n), 1)
    return jnp.sum(jnp.where(eye, jnp.broadcast_to(row, (n, n)), 0.0), axis=1, keepdims=True)


def modulate(kernel_ref, style, affine, main_ref, edge_ref):
    styles = (
        lax.dot_general(
            style, affine, NT, precision=lax.Precision.HIGHEST, preferred_element_type=F32
        )
        + 1.0
    )
    total = jnp.zeros((64, 64), F32)
    for k in range(27):
        scaled = kernel_ref[k].astype(F32) * styles
        total = total + scaled * scaled
    demod = lax.rsqrt(jnp.sum(total, axis=1, keepdims=True) + 1e-08)

    def tap(k):
        return kernel_ref[k].astype(F32) * styles * demod

    zero = jnp.zeros((64, 64), F32)
    for g in range(3):
        for e in range(3):
            for half in range(2):
                k = 9 * e + 6 * half + g
                right = zero if half else tap(k + 3)
                main_ref[pl.ds(64 * g, 64), pl.ds(256 * e + 128 * half, 128)] = jnp.concatenate(
                    [tap(k), right], axis=1
                ).astype(BF16)
    for ef in range(9):
        edge_ref[pl.ds(0, 64), pl.ds(128 * ef, 128)] = jnp.concatenate(
            [zero, tap(3 * ef)], axis=1
        ).astype(BF16)
        edge_ref[pl.ds(64, 64), pl.ds(128 * ef, 128)] = jnp.concatenate(
            [tap(3 * ef + 2), zero], axis=1
        ).astype(BF16)


def pack_edges(cells_ref, pick, edge_ref):
    rows = jnp.concatenate([cells_ref[1 + r // 8, 1 + r % 8] for r in range(16)], axis=1)
    both = lax.dot_general(pick, rows, NT, preferred_element_type=F32)
    edge_ref[...] = jnp.concatenate([both[:16], both[16:]], axis=1).astype(BF16)


def unpack_edges(got_ref, ring_ref):
    lane = lax.broadcasted_iota(jnp.int32, (16, 128), 1)
    for da in (0, -1, 1):
        for db in (0, -1, 1):
            low = got_ref[SIDES.index((da, db, 1))].astype(F32)
            high = got_ref[SIDES.index((da, db, -1))].astype(F32)
            tile = jnp.where(lane < 64, high, low)
            for x in {0: (0, 1), 1: (1,), -1: (0,)}[da]:
                to_x = {0: 1 + x, 1: 0, -1: 3}[da]
                if db == 0:
                    ring_ref[to_x, pl.ds(1, 8)] = tile[8 * x : 8 * x + 8]
                elif db == 1:
                    ring_ref[to_x, pl.ds(0, 1)] = tile[8 * x + 7 : 8 * x + 8]
                else:
                    ring_ref[to_x, pl.ds(9, 1)] = tile[8 * x : 8 * x + 1]


def stack(cells_ref, plane, y, last):
    return jnp.concatenate(
        [
            jnp.concatenate([cells_ref[plane, y + f], cells_ref[plane, y + f + 1]], axis=1)
            for f in range(3)
        ]
        + [last],
        axis=0,
    )


def taps(main_ref, e, stacked):
    return jnp.dot(main_ref[:, pl.ds(256 * e, 256)], stacked, preferred_element_type=F32)


def convolve_own(cells_ref, main_ref, parts_ref):
    zero = jnp.zeros((64, 256), BF16)
    for pair in range(4):
        near = stack(cells_ref, 1, 2 * pair, zero)
        far = stack(cells_ref, 2, 2 * pair, zero)
        parts_ref[pair] = taps(main_ref, 1, near) + taps(main_ref, 2, far)
        parts_ref[4 + pair] = taps(main_ref, 0, near) + taps(main_ref, 1, far)


def convolve_ends(ring_ref, edge_ref, main_ref):
    window = jnp.concatenate(
        [
            jnp.concatenate([ring_ref[e + x, pl.ds(f, 8)] for x in range(2)], axis=0)
            for e in range(3)
            for f in range(3)
        ],
        axis=1,
    ).astype(BF16)
    ends = lax.dot_general(edge_ref[...], window, NT, preferred_element_type=F32)
    high = ends.astype(BF16).astype(F32)
    rest = ends - high
    four = jnp.concatenate([high[:64], high[64:], rest[:64], rest[64:]], axis=1)
    wide = jnp.concatenate([jnp.zeros((64, 64), F32), four], axis=1)
    lane = lax.broadcasted_iota(jnp.int32, (64, 128), 1)
    for e in (0, 2):
        spot = pl.ds(256 * e + 128, 128)
        kept = main_ref[pl.ds(64, 64), spot].astype(F32)
        main_ref[pl.ds(64, 64), spot] = jnp.where(lane < 64, kept, wide).astype(BF16)


def convolve_halo(cells_ref, main_ref, parts_ref, place_ref, emit):
    lane = lax.broadcasted_iota(jnp.int32, (64, 128), 1)
    for pair in range(8):
        x, y = pair // 4, 2 * (pair % 4)
        parts = parts_ref[pair] + taps(main_ref, 2 * x, stack(cells_ref, 3 * x, y, place_ref[pair]))
        for half in range(2):
            row = 8 * x + y + half
            lanes = slice(128 * half, 128 * half + 128)
            low = jnp.where(
                lane == 0, 0.0, pltpu.roll(parts[0:64, lanes], 1, 1)
            )
            high = jnp.where(
                lane == 127, 0.0, pltpu.roll(parts[128:192, lanes], 127, 1)
            )
            emit(row, low + parts[64:128, lanes] + high)


def activate(values):
    return jnp.maximum(values, 0.2 * values) * jnp.sqrt(F32(2.0))


def paint(dest, cells, mass, live, left_ref, right_ref, part_ref):
    block = lax.broadcasted_iota(jnp.int32, (32, 64), 0)
    mass = jnp.where(block < live, mass.astype(F32), 0.0)
    n = dest.shape[1]
    eye = lax.broadcasted_iota(jnp.int32, (n, n), 0) == lax.broadcasted_iota(jnp.int32, (n, n), 1)
    spread = jnp.where(eye, jnp.broadcast_to(dest.astype(F32), (n, n)), 0.0)
    base = jnp.sum(spread, axis=1, keepdims=True).astype(jnp.int32)
    key = base * 2048 + cells
    key = jnp.concatenate([key[:16], key[16:]], axis=1)
    mass = jnp.concatenate([mass[:16], mass[16:]], axis=1)
    upper = key >> 7
    lower = key & 127
    tall = lax.broadcasted_iota(jnp.int32, (512, 128), 0)
    short = lax.broadcasted_iota(jnp.int32, (128, 128), 0)
    for n in range(16):
        lanes = pl.ds(128 * n, 128)
        left_ref[:, lanes] = jnp.where(
            tall == upper[n : n + 1], jnp.broadcast_to(mass[n : n + 1], (512, 128)), 0.0
        ).astype(BF16)
        right_ref[:, lanes] = jnp.where(short == lower[n : n + 1], 1.0, 0.0).astype(BF16)
    painted = lax.dot_general(left_ref[...], right_ref[...], NT, preferred_element_type=F32)
    part_ref[...] = painted.astype(BF16).reshape(32, 16, 128)


def body(sizes, n_in, live_ref, *refs):
    sources = refs[:n_in]
    out_ref = refs[n_in]
    held = refs[n_in + 1 : 2 * n_in + 1]
    (
        left_ref,
        right_ref,
        part_ref,
        sums_ref,
        cells_first,
        cells_second,
        edge_first,
        edge_second,
        got_first,
        got_second,
        ring_ref,
        main_first,
        main_second,
        ends_first,
        ends_second,
        parts_ref,
        place_ref,
        fetch_sem,
        part_sem,
        halo_sem,
        edge_sem,
    ) = refs[2 * n_in + 1 :]
    n_gx, n_gy, n_gz = sizes
    slab = n_gy * n_gz
    me = (lax.axis_index("gx"), lax.axis_index("gy"), lax.axis_index("gz"))
    mine = me[1] * n_gz + me[2]
    at_x = {d: (me[0] + d + n_gx) % n_gx for d in (-1, 0, 1)}
    at_y = [(me[1] + d) % n_gy for d in range(n_gy)]
    at_z = [(me[2] + d) % n_gz for d in range(n_gz)]

    def place(move):
        return (at_x[move[0]], at_y[move[1] % n_gy], at_z[move[2] % n_gz])

    others = [(dy, dz) for dy in range(n_gy) for dz in range(n_gz) if (dy, dz) != (0, 0)]

    fetches = [
        pltpu.make_async_copy(source, kept, fetch_sem.at[n])
        for n, (source, kept) in enumerate(zip(sources, held))
    ]
    for fetch in fetches[:4]:
        fetch.start()
    barrier = pltpu.get_barrier_semaphore()
    for da in (-1, 1):
        for db in (-1, 0, 1):
            for dc in (-1, 0, 1):
                pl.semaphore_signal(
                    barrier, inc=1, device_id=place((da, db, dc)), device_id_type=MESH
                )
    for dy, dz in others:
        pl.semaphore_signal(
            barrier, inc=1, device_id=(me[0], at_y[dy], at_z[dz]), device_id_type=MESH
        )
    for fetch in fetches[4:]:
        fetch.start()

    features, dest, cells, mass, style, *layers = held
    which = lax.broadcasted_iota(jnp.int32, (32, 2048), 0)
    spot = lax.broadcasted_iota(jnp.int32, (32, 2048), 1)
    wanted = (which % 16) * 128 + (which // 16) * 127
    pick = jnp.where(spot == wanted, 1.0, 0.0).astype(BF16)

    fetches[0].wait()
    for x in range(2):
        turned = jnp.transpose(features[:, x].astype(F32), (1, 0, 2))
        cells_first[1 + x, pl.ds(1, 8)] = turned.astype(BF16)
    pack_edges(cells_first, pick, edge_first)

    pl.semaphore_wait(barrier, slab - 1 + 18)

    def start_halo(layer, cells_ref, edge_ref, got_ref):
        for n, move in enumerate(SIDES):
            pltpu.make_async_remote_copy(
                src_ref=edge_ref,
                dst_ref=got_ref.at[n],
                send_sem=edge_sem.at[layer, 0],
                recv_sem=edge_sem.at[layer, 1],
                device_id=place(move),
                device_id_type=MESH,
            ).start()
        for da, db in PLANAR:
            group = 0 if da == 0 else 2
            src_x = {1: pl.ds(2, 1), -1: pl.ds(1, 1), 0: pl.ds(1, 2)}[da]
            dst_x = {1: pl.ds(0, 1), -1: pl.ds(3, 1), 0: pl.ds(1, 2)}[da]
            src_y = {1: pl.ds(8, 1), -1: pl.ds(1, 1), 0: pl.ds(1, 8)}[db]
            dst_y = {1: pl.ds(0, 1), -1: pl.ds(9, 1), 0: pl.ds(1, 8)}[db]
            pltpu.make_async_remote_copy(
                src_ref=cells_ref.at[src_x, src_y],
                dst_ref=cells_ref.at[dst_x, dst_y],
                send_sem=halo_sem.at[layer, group],
                recv_sem=halo_sem.at[layer, group + 1],
                device_id=place((da, db, 0)),
                device_id_type=MESH,
            ).start()

    def wait_for(ref, sem):
        pltpu.make_async_copy(ref, ref, sem).wait()

    def wait_beside(layer, cells_ref):
        four = cells_ref.at[pl.ds(0, 1), pl.ds(0, 4)]
        wait_for(four, halo_sem.at[layer, 1])

    def wait_across(layer, cells_ref):
        twenty = cells_ref.at[pl.ds(0, 2), pl.ds(0, 10)]
        wait_for(twenty, halo_sem.at[layer, 3])

    def wait_edges(layer, got_ref):
        wait_for(got_ref, edge_sem.at[layer, 1])

    def wait_sent(layer, cells_ref, got_ref):
        wait_for(cells_ref.at[pl.ds(0, 1), pl.ds(0, 4)], halo_sem.at[layer, 0])
        wait_for(cells_ref.at[pl.ds(0, 2), pl.ds(0, 10)], halo_sem.at[layer, 2])
        wait_for(got_ref, edge_sem.at[layer, 0])

    start_halo(0, cells_first, edge_first, got_first)
    for fetch in fetches[1:4]:
        fetch.wait()
    paint(dest[...], cells[...], mass[...], live_ref[0], left_ref, right_ref, part_ref)
    sums_ref[pl.ds(mine, 1)] = part_ref[pl.ds(mine, 1)]
    for dy, dz in others:
        pltpu.make_async_remote_copy(
            src_ref=part_ref.at[at_y[dy] * n_gz + at_z[dz]],
            dst_ref=sums_ref.at[mine],
            send_sem=part_sem.at[0],
            recv_sem=part_sem.at[1],
            device_id=(me[0], at_y[dy], at_z[dz]),
            device_id_type=MESH,
        ).start()


    nth = lax.broadcasted_iota(jnp.int32, (64, 256), 0) % 32
    lane = lax.broadcasted_iota(jnp.int32, (64, 256), 1)
    for pair in range(8):
        target = 128 * (nth % 2) + 127 * (nth // 16)
        hit = (nth % 16 // 2 == pair) & (lane == target)
        place_ref[pair] = jnp.where(hit, 1.0, 0.0).astype(BF16)
    for fetch in fetches[4:]:
        fetch.wait()
    style = style[...]
    modulate(layers[1], style, layers[0][...], main_first, ends_first)
    modulate(layers[5], style, layers[4][...], main_second, ends_second)
    bias_first, gain_first, bias_second, gain_second = (
        jnp.broadcast_to(column(layers[n][...]), (64, 128)) for n in (2, 3, 6, 7)
    )

    wait_beside(0, cells_first)
    convolve_own(cells_first, main_first, parts_ref)
    wait_edges(0, got_first)
    unpack_edges(got_first, ring_ref)
    convolve_ends(ring_ref, ends_first, main_first)
    rest = sums_ref.at[pl.ds(0, slab - 1)]
    wait_for(rest, part_sem.at[1])
    density = sums_ref[0].astype(F32)
    for n in range(1, slab):
        density = density + sums_ref[n].astype(F32)
    wait_across(0, cells_first)

    def keep(row, values):
        cells_second[1 + row // 8, 1 + row % 8] = activate(
            values + gain_first * density[row : row + 1] + bias_first
        ).astype(BF16)

    convolve_halo(cells_first, main_first, parts_ref, place_ref, keep)
    pack_edges(cells_second, pick, edge_second)
    start_halo(1, cells_second, edge_second, got_second)
    wait_beside(1, cells_second)
    convolve_own(cells_second, main_second, parts_ref)
    wait_edges(1, got_second)
    unpack_edges(got_second, ring_ref)
    convolve_ends(ring_ref, ends_second, main_second)
    wait_across(1, cells_second)

    def finish(row, values):
        out_ref[row // 8, row % 8] = activate(
            values + gain_second * density[row : row + 1] + bias_second
        ).astype(BF16)

    convolve_halo(cells_second, main_second, parts_ref, place_ref, finish)
    wait_for(rest, part_sem.at[0])
    wait_sent(0, cells_first, got_first)
    wait_sent(1, cells_second, got_second)


def shards(sizes, features, dest, cells, masses, live, style, *layers):
    slab = sizes[1] * sizes[2]
    operands = [
        features,
        dest.reshape(1, -1),
        cells,
        masses,
        style.reshape(1, -1),
    ]
    for affine, kernel, bias, gain in (layers[:4], layers[4:]):
        operands += [affine.T, kernel, bias.reshape(1, -1), gain.reshape(1, -1)]
    operands = [pltpu.with_memory_space_constraint(x, pltpu.HBM) for x in operands]
    result = pl.pallas_call(
        functools.partial(body, sizes, len(operands)),
        out_shape=pltpu.VMEM((2, 8, 64, 128), BF16),
        in_specs=[pl.BlockSpec(memory_space=pltpu.SMEM)]
        + [pl.BlockSpec(memory_space=pltpu.HBM)] * len(operands),
        out_specs=pl.BlockSpec(memory_space=pltpu.VMEM),
        scratch_shapes=[pltpu.VMEM(x.shape, x.dtype) for x in operands]
        + [
            pltpu.VMEM((512, 2048), BF16),
            pltpu.VMEM((128, 2048), BF16),
            pltpu.VMEM((slab, 16, 128), BF16),
            pltpu.VMEM((slab, 16, 128), BF16),
            pltpu.VMEM((4, 10, 64, 128), BF16),
            pltpu.VMEM((4, 10, 64, 128), BF16),
            pltpu.VMEM((16, 128), BF16),
            pltpu.VMEM((16, 128), BF16),
            pltpu.VMEM((18, 16, 128), BF16),
            pltpu.VMEM((18, 16, 128), BF16),
            pltpu.VMEM((4, 16, 128), F32),
            pltpu.VMEM((192, 768), BF16),
            pltpu.VMEM((192, 768), BF16),
            pltpu.VMEM((128, 1152), BF16),
            pltpu.VMEM((128, 1152), BF16),
            pltpu.VMEM((8, 192, 256), F32),
            pltpu.VMEM((8, 64, 256), BF16),
            pltpu.SemaphoreType.DMA((len(operands),)),
            pltpu.SemaphoreType.DMA((2,)),
            pltpu.SemaphoreType.DMA((2, 4)),
            pltpu.SemaphoreType.DMA((2, 2)),
        ],
        compiler_params=pltpu.CompilerParams(
            collective_id=0, has_side_effects=True, vmem_limit_bytes=40 * 1024 * 1024
        ),
        name="styled_block",
    )(live, *operands)
    return result.transpose(2, 0, 1, 3)


def solution(mesh):
    sizes = (mesh.shape["gx"], mesh.shape["gy"], mesh.shape["gz"])
    spread = P(("gx", "gy", "gz"), None)
    return jax.shard_map(
        functools.partial(shards, sizes),
        mesh=mesh,
        in_specs=(P(None, "gx", "gy", "gz"), spread, spread, spread, P(("gx", "gy", "gz")))
        + (P(),) * 9,
        out_specs=P(None, "gx", "gy", "gz"),
        check_vma=False,
    )
```

```python
import functools

import jax
import jax.numpy as jnp
from jax import lax
from jax.experimental import pallas as pl
from jax.experimental.pallas import tpu as pltpu
from jax.sharding import PartitionSpec as P

MESH = pl.DeviceIdType.MESH
F32 = jnp.float32
BF16 = jnp.bfloat16
NT = (((1,), (1,)), ((), ()))
SIDES = [(da, db, dc) for da in (-1, 1, 0) for db in (-1, 1, 0) for dc in (-1, 1)]
PLANAR = [(1, 1), (1, -1), (-1, 1), (-1, -1), (0, 1), (0, -1), (1, 0), (-1, 0)]


def column(row):
    n = row.shape[1]
    eye = lax.broadcasted_iota(jnp.int32, (n, n), 0) == lax.broadcasted_iota(jnp.int32, (n, n), 1)
    return jnp.sum(jnp.where(eye, jnp.broadcast_to(row, (n, n)), 0.0), axis=1, keepdims=True)


def modulate(kernel_ref, style, affine, main_ref, edge_ref):
    styles = (
        lax.dot_general(
            style, affine, NT, precision=lax.Precision.HIGHEST, preferred_element_type=F32
        )
        + 1.0
    )
    total = jnp.zeros((64, 64), F32)
    for k in range(27):
        scaled = kernel_ref[k].astype(F32) * styles
        total = total + scaled * scaled
    demod = lax.rsqrt(jnp.sum(total, axis=1, keepdims=True) + 1e-08)

    def tap(k):
        return kernel_ref[k].astype(F32) * styles * demod

    zero = jnp.zeros((64, 64), F32)
    for g in range(3):
        for e in range(3):
            for half in range(2):
                k = 9 * e + 6 * half + g
                right = zero if half else tap(k + 3)
                main_ref[pl.ds(64 * g, 64), pl.ds(256 * e + 128 * half, 128)] = jnp.concatenate(
                    [tap(k), right], axis=1
                ).astype(BF16)
    for ef in range(9):
        edge_ref[pl.ds(0, 64), pl.ds(128 * ef, 128)] = jnp.concatenate(
            [zero, tap(3 * ef)], axis=1
        ).astype(BF16)
        edge_ref[pl.ds(64, 64), pl.ds(128 * ef, 128)] = jnp.concatenate(
            [tap(3 * ef + 2), zero], axis=1
        ).astype(BF16)


def pack_edges(cells_ref, pick, edge_ref):
    rows = jnp.concatenate([cells_ref[1 + r // 8, 1 + r % 8] for r in range(16)], axis=1)
    both = lax.dot_general(pick, rows, NT, preferred_element_type=F32)
    edge_ref[...] = jnp.concatenate([both[:16], both[16:]], axis=1).astype(BF16)


def unpack_edges(got_ref, ring_ref):
    lane = lax.broadcasted_iota(jnp.int32, (16, 128), 1)
    for da in (0, -1, 1):
        for db in (0, -1, 1):
            low = got_ref[SIDES.index((da, db, 1))].astype(F32)
            high = got_ref[SIDES.index((da, db, -1))].astype(F32)
            tile = jnp.where(lane < 64, high, low)
            for x in {0: (0, 1), 1: (1,), -1: (0,)}[da]:
                to_x = {0: 1 + x, 1: 0, -1: 3}[da]
                if db == 0:
                    ring_ref[to_x, pl.ds(1, 8)] = tile[8 * x : 8 * x + 8]
                elif db == 1:
                    ring_ref[to_x, pl.ds(0, 1)] = tile[8 * x + 7 : 8 * x + 8]
                else:
                    ring_ref[to_x, pl.ds(9, 1)] = tile[8 * x : 8 * x + 1]


def stack(cells_ref, plane, y, last):
    return jnp.concatenate(
        [
            jnp.concatenate([cells_ref[plane, y + f], cells_ref[plane, y + f + 1]], axis=1)
            for f in range(3)
        ]
        + [last],
        axis=0,
    )


def taps(main_ref, e, stacked):
    return jnp.dot(main_ref[:, pl.ds(256 * e, 256)], stacked, preferred_element_type=F32)


def convolve_own(cells_ref, main_ref, parts_ref):
    zero = jnp.zeros((64, 256), BF16)
    for pair in range(4):
        near = stack(cells_ref, 1, 2 * pair, zero)
        far = stack(cells_ref, 2, 2 * pair, zero)
        parts_ref[pair] = taps(main_ref, 1, near) + taps(main_ref, 2, far)
        parts_ref[4 + pair] = taps(main_ref, 0, near) + taps(main_ref, 1, far)


def convolve_ends(ring_ref, edge_ref, main_ref):
    window = jnp.concatenate(
        [
            jnp.concatenate([ring_ref[e + x, pl.ds(f, 8)] for x in range(2)], axis=0)
            for e in range(3)
            for f in range(3)
        ],
        axis=1,
    ).astype(BF16)
    ends = lax.dot_general(edge_ref[...], window, NT, preferred_element_type=F32)
    high = ends.astype(BF16).astype(F32)
    rest = ends - high
    four = jnp.concatenate([high[:64], high[64:], rest[:64], rest[64:]], axis=1)
    wide = jnp.concatenate([jnp.zeros((64, 64), F32), four], axis=1)
    lane = lax.broadcasted_iota(jnp.int32, (64, 128), 1)
    for e in (0, 2):
        spot = pl.ds(256 * e + 128, 128)
        kept = main_ref[pl.ds(64, 64), spot].astype(F32)
        main_ref[pl.ds(64, 64), spot] = jnp.where(lane < 64, kept, wide).astype(BF16)


def convolve_halo(cells_ref, main_ref, parts_ref, place_ref, emit):
    lane = lax.broadcasted_iota(jnp.int32, (64, 128), 1)
    for pair in range(8):
        x, y = pair // 4, 2 * (pair % 4)
        parts = parts_ref[pair] + taps(main_ref, 2 * x, stack(cells_ref, 3 * x, y, place_ref[pair]))
        for half in range(2):
            row = 8 * x + y + half
            lanes = slice(128 * half, 128 * half + 128)
            low = jnp.where(
                lane == 0, 0.0, pltpu.roll(parts[0:64, lanes], 1, 1)
            )
            high = jnp.where(
                lane == 127, 0.0, pltpu.roll(parts[128:192, lanes], 127, 1)
            )
            emit(row, low + parts[64:128, lanes] + high)


def activate(values):
    return jnp.maximum(values, 0.2 * values) * jnp.sqrt(F32(2.0))


def paint(dest, cells, mass, live, left_ref, right_ref, part_ref):
    block = lax.broadcasted_iota(jnp.int32, (32, 64), 0)
    mass = jnp.where(block < live, mass.astype(F32), 0.0)
    n = dest.shape[1]
    eye = lax.broadcasted_iota(jnp.int32, (n, n), 0) == lax.broadcasted_iota(jnp.int32, (n, n), 1)
    spread = jnp.where(eye, jnp.broadcast_to(dest.astype(F32), (n, n)), 0.0)
    base = jnp.sum(spread, axis=1, keepdims=True).astype(jnp.int32)
    key = base * 2048 + cells
    key = jnp.concatenate([key[:16], key[16:]], axis=1)
    mass = jnp.concatenate([mass[:16], mass[16:]], axis=1)
    upper = key >> 7
    lower = key & 127
    tall = lax.broadcasted_iota(jnp.int32, (512, 128), 0)
    short = lax.broadcasted_iota(jnp.int32, (128, 128), 0)
    for n in range(16):
        lanes = pl.ds(128 * n, 128)
        left_ref[:, lanes] = jnp.where(
            tall == upper[n : n + 1], jnp.broadcast_to(mass[n : n + 1], (512, 128)), 0.0
        ).astype(BF16)
        right_ref[:, lanes] = jnp.where(short == lower[n : n + 1], 1.0, 0.0).astype(BF16)
    painted = lax.dot_general(left_ref[...], right_ref[...], NT, preferred_element_type=F32)
    part_ref[...] = painted.astype(BF16).reshape(32, 16, 128)


def body(sizes, n_in, live_ref, *refs):
    sources = refs[:n_in]
    cells_second, main_second, parts_ref, place_ref, addend_ref = refs[n_in : n_in + 5]
    held = refs[n_in + 5 : 2 * n_in + 5]
    (
        left_ref,
        right_ref,
        part_ref,
        sums_ref,
        cells_first,
        edge_first,
        edge_second,
        got_first,
        got_second,
        ring_ref,
        main_first,
        ends_first,
        ends_second,
        fetch_sem,
        part_sem,
        halo_sem,
        edge_sem,
    ) = refs[2 * n_in + 5 :]
    n_gx, n_gy, n_gz = sizes
    slab = n_gy * n_gz
    me = (lax.axis_index("gx"), lax.axis_index("gy"), lax.axis_index("gz"))
    mine = me[1] * n_gz + me[2]
    at_x = {d: (me[0] + d + n_gx) % n_gx for d in (-1, 0, 1)}
    at_y = [(me[1] + d) % n_gy for d in range(n_gy)]
    at_z = [(me[2] + d) % n_gz for d in range(n_gz)]

    def place(move):
        return (at_x[move[0]], at_y[move[1] % n_gy], at_z[move[2] % n_gz])

    others = [(dy, dz) for dy in range(n_gy) for dz in range(n_gz) if (dy, dz) != (0, 0)]

    fetches = [
        pltpu.make_async_copy(source, kept, fetch_sem.at[n])
        for n, (source, kept) in enumerate(zip(sources, held))
    ]
    for fetch in fetches[:4]:
        fetch.start()
    barrier = pltpu.get_barrier_semaphore()
    for da in (-1, 1):
        for db in (-1, 0, 1):
            for dc in (-1, 0, 1):
                pl.semaphore_signal(
                    barrier, inc=1, device_id=place((da, db, dc)), device_id_type=MESH
                )
    for dy, dz in others:
        pl.semaphore_signal(
            barrier, inc=1, device_id=(me[0], at_y[dy], at_z[dz]), device_id_type=MESH
        )
    for fetch in fetches[4:]:
        fetch.start()

    features, dest, cells, mass, style, *layers = held
    which = lax.broadcasted_iota(jnp.int32, (32, 2048), 0)
    spot = lax.broadcasted_iota(jnp.int32, (32, 2048), 1)
    wanted = (which % 16) * 128 + (which // 16) * 127
    pick = jnp.where(spot == wanted, 1.0, 0.0).astype(BF16)

    fetches[0].wait()
    for x in range(2):
        turned = jnp.transpose(features[:, x].astype(F32), (1, 0, 2))
        cells_first[1 + x, pl.ds(1, 8)] = turned.astype(BF16)
    pack_edges(cells_first, pick, edge_first)

    pl.semaphore_wait(barrier, slab - 1 + 18)

    def start_halo(layer, cells_ref, edge_ref, got_ref):
        for n, move in enumerate(SIDES):
            pltpu.make_async_remote_copy(
                src_ref=edge_ref,
                dst_ref=got_ref.at[n],
                send_sem=edge_sem.at[layer, 0],
                recv_sem=edge_sem.at[layer, 1],
                device_id=place(move),
                device_id_type=MESH,
            ).start()
        for da, db in PLANAR:
            group = 0 if da == 0 else 2
            src_x = {1: pl.ds(2, 1), -1: pl.ds(1, 1), 0: pl.ds(1, 2)}[da]
            dst_x = {1: pl.ds(0, 1), -1: pl.ds(3, 1), 0: pl.ds(1, 2)}[da]
            src_y = {1: pl.ds(8, 1), -1: pl.ds(1, 1), 0: pl.ds(1, 8)}[db]
            dst_y = {1: pl.ds(0, 1), -1: pl.ds(9, 1), 0: pl.ds(1, 8)}[db]
            pltpu.make_async_remote_copy(
                src_ref=cells_ref.at[src_x, src_y],
                dst_ref=cells_ref.at[dst_x, dst_y],
                send_sem=halo_sem.at[layer, group],
                recv_sem=halo_sem.at[layer, group + 1],
                device_id=place((da, db, 0)),
                device_id_type=MESH,
            ).start()

    def wait_for(ref, sem):
        pltpu.make_async_copy(ref, ref, sem).wait()

    def wait_beside(layer, cells_ref):
        four = cells_ref.at[pl.ds(0, 1), pl.ds(0, 4)]
        wait_for(four, halo_sem.at[layer, 1])

    def wait_across(layer, cells_ref):
        twenty = cells_ref.at[pl.ds(0, 2), pl.ds(0, 10)]
        wait_for(twenty, halo_sem.at[layer, 3])

    def wait_edges(layer, got_ref):
        wait_for(got_ref, edge_sem.at[layer, 1])

    def wait_sent(layer, cells_ref, got_ref):
        wait_for(cells_ref.at[pl.ds(0, 1), pl.ds(0, 4)], halo_sem.at[layer, 0])
        wait_for(cells_ref.at[pl.ds(0, 2), pl.ds(0, 10)], halo_sem.at[layer, 2])
        wait_for(got_ref, edge_sem.at[layer, 0])

    start_halo(0, cells_first, edge_first, got_first)
    for fetch in fetches[1:4]:
        fetch.wait()
    paint(dest[...], cells[...], mass[...], live_ref[0], left_ref, right_ref, part_ref)
    sums_ref[pl.ds(mine, 1)] = part_ref[pl.ds(mine, 1)]
    for dy, dz in others:
        pltpu.make_async_remote_copy(
            src_ref=part_ref.at[at_y[dy] * n_gz + at_z[dz]],
            dst_ref=sums_ref.at[mine],
            send_sem=part_sem.at[0],
            recv_sem=part_sem.at[1],
            device_id=(me[0], at_y[dy], at_z[dz]),
            device_id_type=MESH,
        ).start()


    nth = lax.broadcasted_iota(jnp.int32, (64, 256), 0) % 32
    lane = lax.broadcasted_iota(jnp.int32, (64, 256), 1)
    for pair in range(8):
        target = 128 * (nth % 2) + 127 * (nth // 16)
        hit = (nth % 16 // 2 == pair) & (lane == target)
        place_ref[pair] = jnp.where(hit, 1.0, 0.0).astype(BF16)
    for fetch in fetches[4:]:
        fetch.wait()
    style = style[...]
    modulate(layers[1], style, layers[0][...], main_first, ends_first)
    modulate(layers[5], style, layers[4][...], main_second, ends_second)
    bias_first, gain_first, bias_second, gain_second = (
        jnp.broadcast_to(column(layers[n][...]), (64, 128)) for n in (2, 3, 6, 7)
    )

    wait_beside(0, cells_first)
    convolve_own(cells_first, main_first, parts_ref)
    wait_edges(0, got_first)
    unpack_edges(got_first, ring_ref)
    convolve_ends(ring_ref, ends_first, main_first)
    rest = sums_ref.at[pl.ds(0, slab - 1)]
    wait_for(rest, part_sem.at[1])
    density = sums_ref[0].astype(F32)
    for n in range(1, slab):
        density = density + sums_ref[n].astype(F32)
    wait_across(0, cells_first)

    def keep(row, values):
        cells_second[1 + row // 8, 1 + row % 8] = activate(
            values + gain_first * density[row : row + 1] + bias_first
        ).astype(BF16)

    convolve_halo(cells_first, main_first, parts_ref, place_ref, keep)
    pack_edges(cells_second, pick, edge_second)
    start_halo(1, cells_second, edge_second, got_second)
    for row in range(16):
        addend_ref[row] = gain_second * density[row : row + 1] + bias_second
    wait_beside(1, cells_second)
    convolve_own(cells_second, main_second, parts_ref)
    wait_edges(1, got_second)
    unpack_edges(got_second, ring_ref)
    convolve_ends(ring_ref, ends_second, main_second)
    wait_across(1, cells_second)

    wait_for(rest, part_sem.at[0])
    wait_sent(0, cells_first, got_first)
    wait_sent(1, cells_second, got_second)


def last(cells_ref, main_ref, parts_ref, place_ref, addend_ref, out_ref, rows_ref, turned_ref, sems):
    copies = [
        pltpu.make_async_copy(turned_ref.at[x], out_ref.at[:, x], sems.at[x]) for x in range(2)
    ]

    def finish(row, values):
        x = row // 8
        rows_ref[x, row % 8] = activate(values + addend_ref[row])
        if row % 8 == 7:
            turned_ref[x] = jnp.transpose(rows_ref[x], (1, 0, 2)).astype(BF16)
            copies[x].start()

    convolve_halo(cells_ref, main_ref, parts_ref, place_ref, finish)
    for copy in copies:
        copy.wait()


def shards(sizes, features, dest, cells, masses, live, style, *layers):
    slab = sizes[1] * sizes[2]
    operands = [
        features,
        dest.reshape(1, -1),
        cells,
        masses,
        style.reshape(1, -1),
    ]
    for affine, kernel, bias, gain in (layers[:4], layers[4:]):
        operands += [affine.T, kernel, bias.reshape(1, -1), gain.reshape(1, -1)]
    operands = [pltpu.with_memory_space_constraint(x, pltpu.HBM) for x in operands]
    vmem = pl.BlockSpec(memory_space=pltpu.VMEM)
    result = pl.pallas_call(
        functools.partial(body, sizes, len(operands)),
        out_shape=(
            pltpu.VMEM((4, 10, 64, 128), BF16),
            pltpu.VMEM((192, 768), BF16),
            pltpu.VMEM((8, 192, 256), F32),
            pltpu.VMEM((8, 64, 256), BF16),
            pltpu.VMEM((16, 64, 128), F32),
        ),
        in_specs=[pl.BlockSpec(memory_space=pltpu.SMEM)]
        + [pl.BlockSpec(memory_space=pltpu.HBM)] * len(operands),
        out_specs=(pl.BlockSpec(memory_space=pltpu.VMEM),) * 5,
        scratch_shapes=[pltpu.VMEM(x.shape, x.dtype) for x in operands]
        + [
            pltpu.VMEM((512, 2048), BF16),
            pltpu.VMEM((128, 2048), BF16),
            pltpu.VMEM((slab, 16, 128), BF16),
            pltpu.VMEM((slab, 16, 128), BF16),
            pltpu.VMEM((4, 10, 64, 128), BF16),
            pltpu.VMEM((16, 128), BF16),
            pltpu.VMEM((16, 128), BF16),
            pltpu.VMEM((18, 16, 128), BF16),
            pltpu.VMEM((18, 16, 128), BF16),
            pltpu.VMEM((4, 16, 128), F32),
            pltpu.VMEM((192, 768), BF16),
            pltpu.VMEM((128, 1152), BF16),
            pltpu.VMEM((128, 1152), BF16),
            pltpu.SemaphoreType.DMA((len(operands),)),
            pltpu.SemaphoreType.DMA((2,)),
            pltpu.SemaphoreType.DMA((2, 4)),
            pltpu.SemaphoreType.DMA((2, 2)),
        ],
        compiler_params=pltpu.CompilerParams(
            collective_id=0, has_side_effects=True, vmem_limit_bytes=40 * 1024 * 1024
        ),
        name="styled_block",
    )(live, *operands)
    return pl.pallas_call(
        last,
        out_shape=jax.ShapeDtypeStruct((64, 2, 8, 128), BF16),
        in_specs=[vmem] * 5,
        out_specs=pl.BlockSpec(memory_space=pltpu.HBM),
        scratch_shapes=[
            pltpu.VMEM((2, 8, 64, 128), F32),
            pltpu.VMEM((2, 64, 8, 128), BF16),
            pltpu.SemaphoreType.DMA((2,)),
        ],
        name="last_rows",
    )(*(pltpu.with_memory_space_constraint(x, pltpu.VMEM) for x in result))


def solution(mesh):
    sizes = (mesh.shape["gx"], mesh.shape["gy"], mesh.shape["gz"])
    spread = P(("gx", "gy", "gz"), None)
    return jax.shard_map(
        functools.partial(shards, sizes),
        mesh=mesh,
        in_specs=(P(None, "gx", "gy", "gz"), spread, spread, spread, P(("gx", "gy", "gz")))
        + (P(),) * 9,
        out_specs=P(None, "gx", "gy", "gz"),
        check_vma=False,
    )
```

```python
import functools

import jax
import jax.numpy as jnp
from jax import lax
from jax.experimental import pallas as pl
from jax.experimental.pallas import tpu as pltpu
from jax.sharding import PartitionSpec as P

MESH = pl.DeviceIdType.MESH
F32 = jnp.float32
BF16 = jnp.bfloat16
NT = (((1,), (1,)), ((), ()))
SIDES = [(da, db, dc) for da in (-1, 1, 0) for db in (-1, 1, 0) for dc in (-1, 1)]
PLANAR = [(0, 1), (0, -1), (1, 1), (1, -1), (-1, 1), (-1, -1), (1, 0), (-1, 0)]


def column(row):
    n = row.shape[1]
    eye = lax.broadcasted_iota(jnp.int32, (n, n), 0) == lax.broadcasted_iota(jnp.int32, (n, n), 1)
    return jnp.sum(jnp.where(eye, jnp.broadcast_to(row, (n, n)), 0.0), axis=1, keepdims=True)


def modulate(kernel_ref, style, affine, main_ref, edge_ref):
    styles = (
        lax.dot_general(
            style, affine, NT, precision=lax.Precision.HIGHEST, preferred_element_type=F32
        )
        + 1.0
    )
    total = jnp.zeros((64, 64), F32)
    for k in range(27):
        scaled = kernel_ref[k].astype(F32) * styles
        total = total + scaled * scaled
    demod = lax.rsqrt(jnp.sum(total, axis=1, keepdims=True) + 1e-08)

    def tap(k):
        return kernel_ref[k].astype(F32) * styles * demod

    zero = jnp.zeros((64, 64), F32)
    for g in range(3):
        for e in range(3):
            for half in range(2):
                k = 9 * e + 6 * half + g
                right = zero if half else tap(k + 3)
                main_ref[pl.ds(64 * g, 64), pl.ds(256 * e + 128 * half, 128)] = jnp.concatenate(
                    [tap(k), right], axis=1
                ).astype(BF16)
    for ef in range(9):
        edge_ref[pl.ds(0, 64), pl.ds(128 * ef, 128)] = jnp.concatenate(
            [zero, tap(3 * ef)], axis=1
        ).astype(BF16)
        edge_ref[pl.ds(64, 64), pl.ds(128 * ef, 128)] = jnp.concatenate(
            [tap(3 * ef + 2), zero], axis=1
        ).astype(BF16)


def pack_edges(cells_ref, pick, edge_ref):
    rows = jnp.concatenate([cells_ref[1 + r // 8, 1 + r % 8] for r in range(16)], axis=1)
    both = lax.dot_general(pick, rows, NT, preferred_element_type=F32)
    edge_ref[...] = jnp.concatenate([both[:16], both[16:]], axis=1).astype(BF16)


def unpack_edges(got_ref, ring_ref):
    lane = lax.broadcasted_iota(jnp.int32, (16, 128), 1)
    for da in (0, -1, 1):
        for db in (0, -1, 1):
            low = got_ref[SIDES.index((da, db, 1))].astype(F32)
            high = got_ref[SIDES.index((da, db, -1))].astype(F32)
            tile = jnp.where(lane < 64, high, low)
            for x in {0: (0, 1), 1: (1,), -1: (0,)}[da]:
                to_x = {0: 1 + x, 1: 0, -1: 3}[da]
                if db == 0:
                    ring_ref[to_x, pl.ds(1, 8)] = tile[8 * x : 8 * x + 8]
                elif db == 1:
                    ring_ref[to_x, pl.ds(0, 1)] = tile[8 * x + 7 : 8 * x + 8]
                else:
                    ring_ref[to_x, pl.ds(9, 1)] = tile[8 * x : 8 * x + 1]


def stack(cells_ref, plane, y, last):
    return jnp.concatenate(
        [
            jnp.concatenate([cells_ref[plane, y + f], cells_ref[plane, y + f + 1]], axis=1)
            for f in range(3)
        ]
        + [last],
        axis=0,
    )


def taps(main_ref, e, stacked):
    return jnp.dot(main_ref[:, pl.ds(256 * e, 256)], stacked, preferred_element_type=F32)


def convolve_own(cells_ref, main_ref, parts_ref):
    zero = jnp.zeros((64, 256), BF16)
    for pair in range(4):
        near = stack(cells_ref, 1, 2 * pair, zero)
        far = stack(cells_ref, 2, 2 * pair, zero)
        parts_ref[pair] = taps(main_ref, 1, near) + taps(main_ref, 2, far)
        parts_ref[4 + pair] = taps(main_ref, 0, near) + taps(main_ref, 1, far)


def convolve_ends(ring_ref, edge_ref, main_ref):
    window = jnp.concatenate(
        [
            jnp.concatenate([ring_ref[e + x, pl.ds(f, 8)] for x in range(2)], axis=0)
            for e in range(3)
            for f in range(3)
        ],
        axis=1,
    ).astype(BF16)
    ends = lax.dot_general(edge_ref[...], window, NT, preferred_element_type=F32)
    high = ends.astype(BF16).astype(F32)
    rest = ends - high
    four = jnp.concatenate([high[:64], high[64:], rest[:64], rest[64:]], axis=1)
    wide = jnp.concatenate([jnp.zeros((64, 64), F32), four], axis=1)
    lane = lax.broadcasted_iota(jnp.int32, (64, 128), 1)
    for e in (0, 2):
        spot = pl.ds(256 * e + 128, 128)
        kept = main_ref[pl.ds(64, 64), spot].astype(F32)
        main_ref[pl.ds(64, 64), spot] = jnp.where(lane < 64, kept, wide).astype(BF16)


def convolve_halo(cells_ref, main_ref, parts_ref, place_ref, emit):
    lane = lax.broadcasted_iota(jnp.int32, (64, 128), 1)
    for pair in range(8):
        x, y = pair // 4, 2 * (pair % 4)
        parts = parts_ref[pair] + taps(main_ref, 2 * x, stack(cells_ref, 3 * x, y, place_ref[pair]))
        for half in range(2):
            row = 8 * x + y + half
            lanes = slice(128 * half, 128 * half + 128)
            low = jnp.where(
                lane == 0, 0.0, pltpu.roll(parts[0:64, lanes], 1, 1)
            )
            high = jnp.where(
                lane == 127, 0.0, pltpu.roll(parts[128:192, lanes], 127, 1)
            )
            emit(row, low + parts[64:128, lanes] + high)


def activate(values):
    return jnp.maximum(values, 0.2 * values) * jnp.sqrt(F32(2.0))


def paint(dest, cells, mass, live, left_ref, right_ref, part_ref):
    block = lax.broadcasted_iota(jnp.int32, (32, 64), 0)
    mass = jnp.where(block < live, mass.astype(F32), 0.0)
    n = dest.shape[1]
    eye = lax.broadcasted_iota(jnp.int32, (n, n), 0) == lax.broadcasted_iota(jnp.int32, (n, n), 1)
    spread = jnp.where(eye, jnp.broadcast_to(dest.astype(F32), (n, n)), 0.0)
    base = jnp.sum(spread, axis=1, keepdims=True).astype(jnp.int32)
    key = base * 2048 + cells
    key = jnp.concatenate([key[:16], key[16:]], axis=1)
    mass = jnp.concatenate([mass[:16], mass[16:]], axis=1)
    upper = key >> 7
    lower = key & 127
    tall = lax.broadcasted_iota(jnp.int32, (512, 128), 0)
    short = lax.broadcasted_iota(jnp.int32, (128, 128), 0)
    for n in range(16):
        lanes = pl.ds(128 * n, 128)
        left_ref[:, lanes] = jnp.where(
            tall == upper[n : n + 1], jnp.broadcast_to(mass[n : n + 1], (512, 128)), 0.0
        ).astype(BF16)
        right_ref[:, lanes] = jnp.where(short == lower[n : n + 1], 1.0, 0.0).astype(BF16)
    painted = lax.dot_general(left_ref[...], right_ref[...], NT, preferred_element_type=F32)
    part_ref[...] = painted.astype(BF16).reshape(32, 16, 128)


def body(sizes, n_in, live_ref, *refs):
    sources = refs[:n_in]
    cells_second, main_second, parts_ref, place_ref, addend_ref = refs[n_in : n_in + 5]
    held = refs[n_in + 5 : 2 * n_in + 5]
    (
        left_ref,
        right_ref,
        part_ref,
        sums_ref,
        cells_first,
        edge_first,
        edge_second,
        got_first,
        got_second,
        ring_ref,
        main_first,
        ends_first,
        ends_second,
        fetch_sem,
        part_sem,
        halo_sem,
        edge_sem,
    ) = refs[2 * n_in + 5 :]
    n_gx, n_gy, n_gz = sizes
    slab = n_gy * n_gz
    me = (lax.axis_index("gx"), lax.axis_index("gy"), lax.axis_index("gz"))
    mine = me[1] * n_gz + me[2]
    at_x = {d: (me[0] + d + n_gx) % n_gx for d in (-1, 0, 1)}
    at_y = [(me[1] + d) % n_gy for d in range(n_gy)]
    at_z = [(me[2] + d) % n_gz for d in range(n_gz)]

    def place(move):
        return (at_x[move[0]], at_y[move[1] % n_gy], at_z[move[2] % n_gz])

    others = [(dy, dz) for dy in range(n_gy) for dz in range(n_gz) if (dy, dz) != (0, 0)]

    fetches = [
        pltpu.make_async_copy(source, kept, fetch_sem.at[n])
        for n, (source, kept) in enumerate(zip(sources, held))
    ]
    for fetch in fetches[:4]:
        fetch.start()
    barrier = pltpu.get_barrier_semaphore()
    for da in (-1, 1):
        for db in (-1, 0, 1):
            for dc in (-1, 0, 1):
                pl.semaphore_signal(
                    barrier, inc=1, device_id=place((da, db, dc)), device_id_type=MESH
                )
    for dy, dz in others:
        pl.semaphore_signal(
            barrier, inc=1, device_id=(me[0], at_y[dy], at_z[dz]), device_id_type=MESH
        )
    for fetch in fetches[4:]:
        fetch.start()

    features, dest, cells, mass, style, *layers = held
    which = lax.broadcasted_iota(jnp.int32, (32, 2048), 0)
    spot = lax.broadcasted_iota(jnp.int32, (32, 2048), 1)
    wanted = (which % 16) * 128 + (which // 16) * 127
    pick = jnp.where(spot == wanted, 1.0, 0.0).astype(BF16)

    fetches[0].wait()
    for x in range(2):
        turned = jnp.transpose(features[:, x].astype(F32), (1, 0, 2))
        cells_first[1 + x, pl.ds(1, 8)] = turned.astype(BF16)
    pack_edges(cells_first, pick, edge_first)

    pl.semaphore_wait(barrier, slab - 1 + 18)

    def start_halo(layer, cells_ref, edge_ref, got_ref):
        for n, move in enumerate(SIDES):
            pltpu.make_async_remote_copy(
                src_ref=edge_ref,
                dst_ref=got_ref.at[n],
                send_sem=edge_sem.at[layer, 0],
                recv_sem=edge_sem.at[layer, 1],
                device_id=place(move),
                device_id_type=MESH,
            ).start()
        for da, db in PLANAR:
            group = 0 if da == 0 else 2
            src_x = {1: pl.ds(2, 1), -1: pl.ds(1, 1), 0: pl.ds(1, 2)}[da]
            dst_x = {1: pl.ds(0, 1), -1: pl.ds(3, 1), 0: pl.ds(1, 2)}[da]
            src_y = {1: pl.ds(8, 1), -1: pl.ds(1, 1), 0: pl.ds(1, 8)}[db]
            dst_y = {1: pl.ds(0, 1), -1: pl.ds(9, 1), 0: pl.ds(1, 8)}[db]
            pltpu.make_async_remote_copy(
                src_ref=cells_ref.at[src_x, src_y],
                dst_ref=cells_ref.at[dst_x, dst_y],
                send_sem=halo_sem.at[layer, group],
                recv_sem=halo_sem.at[layer, group + 1],
                device_id=place((da, db, 0)),
                device_id_type=MESH,
            ).start()

    def wait_for(ref, sem):
        pltpu.make_async_copy(ref, ref, sem).wait()

    def wait_beside(layer, cells_ref):
        four = cells_ref.at[pl.ds(0, 1), pl.ds(0, 4)]
        wait_for(four, halo_sem.at[layer, 1])

    def wait_across(layer, cells_ref):
        twenty = cells_ref.at[pl.ds(0, 2), pl.ds(0, 10)]
        wait_for(twenty, halo_sem.at[layer, 3])

    def wait_edges(layer, got_ref):
        wait_for(got_ref, edge_sem.at[layer, 1])

    def wait_sent(layer, cells_ref, got_ref):
        wait_for(cells_ref.at[pl.ds(0, 1), pl.ds(0, 4)], halo_sem.at[layer, 0])
        wait_for(cells_ref.at[pl.ds(0, 2), pl.ds(0, 10)], halo_sem.at[layer, 2])
        wait_for(got_ref, edge_sem.at[layer, 0])

    start_halo(0, cells_first, edge_first, got_first)
    for fetch in fetches[1:4]:
        fetch.wait()
    paint(dest[...], cells[...], mass[...], live_ref[0], left_ref, right_ref, part_ref)
    sums_ref[pl.ds(mine, 1)] = part_ref[pl.ds(mine, 1)]
    for dy, dz in others:
        pltpu.make_async_remote_copy(
            src_ref=part_ref.at[at_y[dy] * n_gz + at_z[dz]],
            dst_ref=sums_ref.at[mine],
            send_sem=part_sem.at[0],
            recv_sem=part_sem.at[1],
            device_id=(me[0], at_y[dy], at_z[dz]),
            device_id_type=MESH,
        ).start()


    nth = lax.broadcasted_iota(jnp.int32, (64, 256), 0) % 32
    lane = lax.broadcasted_iota(jnp.int32, (64, 256), 1)
    for pair in range(8):
        target = 128 * (nth % 2) + 127 * (nth // 16)
        hit = (nth % 16 // 2 == pair) & (lane == target)
        place_ref[pair] = jnp.where(hit, 1.0, 0.0).astype(BF16)
    for fetch in fetches[4:]:
        fetch.wait()
    style = style[...]
    modulate(layers[1], style, layers[0][...], main_first, ends_first)
    modulate(layers[5], style, layers[4][...], main_second, ends_second)
    bias_first, gain_first, bias_second, gain_second = (
        jnp.broadcast_to(column(layers[n][...]), (64, 128)) for n in (2, 3, 6, 7)
    )

    wait_beside(0, cells_first)
    convolve_own(cells_first, main_first, parts_ref)
    wait_edges(0, got_first)
    unpack_edges(got_first, ring_ref)
    convolve_ends(ring_ref, ends_first, main_first)
    rest = sums_ref.at[pl.ds(0, slab - 1)]
    wait_for(rest, part_sem.at[1])
    density = sums_ref[0].astype(F32)
    for n in range(1, slab):
        density = density + sums_ref[n].astype(F32)
    for row in range(16):
        addend_ref[row] = gain_first * density[row : row + 1] + bias_first
    wait_across(0, cells_first)

    def keep(row, values):
        cells_second[1 + row // 8, 1 + row % 8] = activate(
            values + addend_ref[row]
        ).astype(BF16)

    convolve_halo(cells_first, main_first, parts_ref, place_ref, keep)
    pack_edges(cells_second, pick, edge_second)
    start_halo(1, cells_second, edge_second, got_second)
    for row in range(16):
        addend_ref[row] = gain_second * density[row : row + 1] + bias_second
    wait_beside(1, cells_second)
    convolve_own(cells_second, main_second, parts_ref)
    wait_edges(1, got_second)
    unpack_edges(got_second, ring_ref)
    convolve_ends(ring_ref, ends_second, main_second)
    wait_across(1, cells_second)

    wait_for(rest, part_sem.at[0])
    wait_sent(0, cells_first, got_first)
    wait_sent(1, cells_second, got_second)


def last(cells_ref, main_ref, parts_ref, place_ref, addend_ref, out_ref, rows_ref, turned_ref, sems):
    copies = [
        pltpu.make_async_copy(turned_ref.at[x], out_ref.at[:, x], sems.at[x]) for x in range(2)
    ]

    def finish(row, values):
        x = row // 8
        rows_ref[x, row % 8] = activate(values + addend_ref[row])
        if row % 8 == 7:
            turned_ref[x] = jnp.transpose(rows_ref[x], (1, 0, 2)).astype(BF16)
            copies[x].start()

    convolve_halo(cells_ref, main_ref, parts_ref, place_ref, finish)
    for copy in copies:
        copy.wait()


def shards(sizes, features, dest, cells, masses, live, style, *layers):
    slab = sizes[1] * sizes[2]
    operands = [
        features,
        dest.reshape(1, -1),
        cells,
        masses,
        style.reshape(1, -1),
    ]
    for affine, kernel, bias, gain in (layers[:4], layers[4:]):
        operands += [affine.T, kernel, bias.reshape(1, -1), gain.reshape(1, -1)]
    operands = [pltpu.with_memory_space_constraint(x, pltpu.HBM) for x in operands]
    vmem = pl.BlockSpec(memory_space=pltpu.VMEM)
    result = pl.pallas_call(
        functools.partial(body, sizes, len(operands)),
        out_shape=(
            pltpu.VMEM((4, 10, 64, 128), BF16),
            pltpu.VMEM((192, 768), BF16),
            pltpu.VMEM((8, 192, 256), F32),
            pltpu.VMEM((8, 64, 256), BF16),
            pltpu.VMEM((16, 64, 128), F32),
        ),
        in_specs=[pl.BlockSpec(memory_space=pltpu.SMEM)]
        + [pl.BlockSpec(memory_space=pltpu.HBM)] * len(operands),
        out_specs=(pl.BlockSpec(memory_space=pltpu.VMEM),) * 5,
        scratch_shapes=[pltpu.VMEM(x.shape, x.dtype) for x in operands]
        + [
            pltpu.VMEM((512, 2048), BF16),
            pltpu.VMEM((128, 2048), BF16),
            pltpu.VMEM((slab, 16, 128), BF16),
            pltpu.VMEM((slab, 16, 128), BF16),
            pltpu.VMEM((4, 10, 64, 128), BF16),
            pltpu.VMEM((16, 128), BF16),
            pltpu.VMEM((16, 128), BF16),
            pltpu.VMEM((18, 16, 128), BF16),
            pltpu.VMEM((18, 16, 128), BF16),
            pltpu.VMEM((4, 16, 128), F32),
            pltpu.VMEM((192, 768), BF16),
            pltpu.VMEM((128, 1152), BF16),
            pltpu.VMEM((128, 1152), BF16),
            pltpu.SemaphoreType.DMA((len(operands),)),
            pltpu.SemaphoreType.DMA((2,)),
            pltpu.SemaphoreType.DMA((2, 4)),
            pltpu.SemaphoreType.DMA((2, 2)),
        ],
        compiler_params=pltpu.CompilerParams(
            collective_id=0, has_side_effects=True, vmem_limit_bytes=40 * 1024 * 1024
        ),
        name="styled_block",
    )(live, *operands)
    return pl.pallas_call(
        last,
        out_shape=jax.ShapeDtypeStruct((64, 2, 8, 128), BF16),
        in_specs=[vmem] * 5,
        out_specs=pl.BlockSpec(memory_space=pltpu.HBM),
        scratch_shapes=[
            pltpu.VMEM((2, 8, 64, 128), F32),
            pltpu.VMEM((2, 64, 8, 128), BF16),
            pltpu.SemaphoreType.DMA((2,)),
        ],
        name="last_rows",
    )(*(pltpu.with_memory_space_constraint(x, pltpu.VMEM) for x in result))


def solution(mesh):
    sizes = (mesh.shape["gx"], mesh.shape["gy"], mesh.shape["gz"])
    spread = P(("gx", "gy", "gz"), None)
    return jax.shard_map(
        functools.partial(shards, sizes),
        mesh=mesh,
        in_specs=(P(None, "gx", "gy", "gz"), spread, spread, spread, P(("gx", "gy", "gz")))
        + (P(),) * 9,
        out_specs=P(None, "gx", "gy", "gz"),
        check_vma=False,
    )
```

```python
import functools

import jax
import jax.numpy as jnp
from jax import lax
from jax.experimental import pallas as pl
from jax.experimental.pallas import tpu as pltpu
from jax.sharding import PartitionSpec as P

MESH = pl.DeviceIdType.MESH
F32 = jnp.float32
BF16 = jnp.bfloat16
NT = (((1,), (1,)), ((), ()))
SIDES = [(da, db, dc) for da in (-1, 1, 0) for db in (-1, 1, 0) for dc in (-1, 1)]
PLANAR = [(1, 1), (1, -1), (-1, 1), (-1, -1), (0, 1), (0, -1), (1, 0), (-1, 0)]


def column(row):
    n = row.shape[1]
    eye = lax.broadcasted_iota(jnp.int32, (n, n), 0) == lax.broadcasted_iota(jnp.int32, (n, n), 1)
    return jnp.sum(jnp.where(eye, jnp.broadcast_to(row, (n, n)), 0.0), axis=1, keepdims=True)


def modulate(kernel_ref, style, affine, main_ref, edge_ref):
    styles = (
        lax.dot_general(
            style, affine, NT, precision=lax.Precision.HIGHEST, preferred_element_type=F32
        )
        + 1.0
    )
    total = jnp.zeros((64, 64), F32)
    for k in range(27):
        scaled = kernel_ref[k].astype(F32) * styles
        total = total + scaled * scaled
    demod = lax.rsqrt(jnp.sum(total, axis=1, keepdims=True) + 1e-08)

    def tap(k):
        return kernel_ref[k].astype(F32) * styles * demod

    zero = jnp.zeros((64, 64), F32)
    for g in range(3):
        for e in range(3):
            for half in range(2):
                k = 9 * e + 6 * half + g
                right = zero if half else tap(k + 3)
                main_ref[pl.ds(64 * g, 64), pl.ds(256 * e + 128 * half, 128)] = jnp.concatenate(
                    [tap(k), right], axis=1
                ).astype(BF16)
    for ef in range(9):
        edge_ref[pl.ds(0, 64), pl.ds(128 * ef, 128)] = jnp.concatenate(
            [zero, tap(3 * ef)], axis=1
        ).astype(BF16)
        edge_ref[pl.ds(64, 64), pl.ds(128 * ef, 128)] = jnp.concatenate(
            [tap(3 * ef + 2), zero], axis=1
        ).astype(BF16)


def pack_edges(cells_ref, pick, edge_ref):
    rows = jnp.concatenate([cells_ref[1 + r // 8, 1 + r % 8] for r in range(16)], axis=1)
    both = lax.dot_general(pick, rows, NT, preferred_element_type=F32)
    edge_ref[...] = jnp.concatenate([both[:16], both[16:]], axis=1).astype(BF16)


def unpack_edges(got_ref, ring_ref):
    lane = lax.broadcasted_iota(jnp.int32, (16, 128), 1)
    for da in (0, -1, 1):
        for db in (0, -1, 1):
            low = got_ref[SIDES.index((da, db, 1))].astype(F32)
            high = got_ref[SIDES.index((da, db, -1))].astype(F32)
            tile = jnp.where(lane < 64, high, low)
            for x in {0: (0, 1), 1: (1,), -1: (0,)}[da]:
                to_x = {0: 1 + x, 1: 0, -1: 3}[da]
                if db == 0:
                    ring_ref[to_x, pl.ds(1, 8)] = tile[8 * x : 8 * x + 8]
                elif db == 1:
                    ring_ref[to_x, pl.ds(0, 1)] = tile[8 * x + 7 : 8 * x + 8]
                else:
                    ring_ref[to_x, pl.ds(9, 1)] = tile[8 * x : 8 * x + 1]


def stack(cells_ref, plane, y, last):
    return jnp.concatenate(
        [
            jnp.concatenate([cells_ref[plane, y + f], cells_ref[plane, y + f + 1]], axis=1)
            for f in range(3)
        ]
        + [last],
        axis=0,
    )


def taps(main_ref, e, stacked):
    return jnp.dot(main_ref[:, pl.ds(256 * e, 256)], stacked, preferred_element_type=F32)


def convolve_own(cells_ref, main_ref, parts_ref):
    zero = jnp.zeros((64, 256), BF16)
    for pair in range(4):
        near = stack(cells_ref, 1, 2 * pair, zero)
        far = stack(cells_ref, 2, 2 * pair, zero)
        parts_ref[pair] = taps(main_ref, 1, near) + taps(main_ref, 2, far)
        parts_ref[4 + pair] = taps(main_ref, 0, near) + taps(main_ref, 1, far)


def convolve_ends(ring_ref, edge_ref, main_ref):
    window = jnp.concatenate(
        [
            jnp.concatenate([ring_ref[e + x, pl.ds(f, 8)] for x in range(2)], axis=0)
            for e in range(3)
            for f in range(3)
        ],
        axis=1,
    ).astype(BF16)
    ends = lax.dot_general(edge_ref[...], window, NT, preferred_element_type=F32)
    high = ends.astype(BF16).astype(F32)
    rest = ends - high
    four = jnp.concatenate([high[:64], high[64:], rest[:64], rest[64:]], axis=1)
    wide = jnp.concatenate([jnp.zeros((64, 64), F32), four], axis=1)
    lane = lax.broadcasted_iota(jnp.int32, (64, 128), 1)
    for e in (0, 2):
        spot = pl.ds(256 * e + 128, 128)
        kept = main_ref[pl.ds(64, 64), spot].astype(F32)
        main_ref[pl.ds(64, 64), spot] = jnp.where(lane < 64, kept, wide).astype(BF16)


def convolve_halo(cells_ref, main_ref, parts_ref, place_ref, emit):
    lane = lax.broadcasted_iota(jnp.int32, (64, 128), 1)
    for pair in range(8):
        x, y = pair // 4, 2 * (pair % 4)
        parts = parts_ref[pair] + taps(main_ref, 2 * x, stack(cells_ref, 3 * x, y, place_ref[pair]))
        for half in range(2):
            row = 8 * x + y + half
            lanes = slice(128 * half, 128 * half + 128)
            low = jnp.where(
                lane == 0, 0.0, pltpu.roll(parts[0:64, lanes], 1, 1)
            )
            high = jnp.where(
                lane == 127, 0.0, pltpu.roll(parts[128:192, lanes], 127, 1)
            )
            emit(row, low + parts[64:128, lanes] + high)


def activate(values):
    return jnp.maximum(values, 0.2 * values) * jnp.sqrt(F32(2.0))


def paint(dest, cells, mass, live, left_ref, right_ref, part_ref):
    block = lax.broadcasted_iota(jnp.int32, (32, 64), 0)
    mass = jnp.where(block < live, mass.astype(F32), 0.0)
    n = dest.shape[1]
    eye = lax.broadcasted_iota(jnp.int32, (n, n), 0) == lax.broadcasted_iota(jnp.int32, (n, n), 1)
    spread = jnp.where(eye, jnp.broadcast_to(dest.astype(F32), (n, n)), 0.0)
    base = jnp.sum(spread, axis=1, keepdims=True).astype(jnp.int32)
    key = base * 2048 + cells
    key = jnp.concatenate([key[:16], key[16:]], axis=1)
    mass = jnp.concatenate([mass[:16], mass[16:]], axis=1)
    upper = key >> 7
    lower = key & 127
    tall = lax.broadcasted_iota(jnp.int32, (512, 128), 0)
    short = lax.broadcasted_iota(jnp.int32, (128, 128), 0)
    for n in range(16):
        lanes = pl.ds(128 * n, 128)
        left_ref[:, lanes] = jnp.where(
            tall == upper[n : n + 1], jnp.broadcast_to(mass[n : n + 1], (512, 128)), 0.0
        ).astype(BF16)
        right_ref[:, lanes] = jnp.where(short == lower[n : n + 1], 1.0, 0.0).astype(BF16)
    painted = lax.dot_general(left_ref[...], right_ref[...], NT, preferred_element_type=F32)
    part_ref[...] = painted.astype(BF16).reshape(32, 16, 128)


def body(sizes, n_in, live_ref, *refs):
    sources = refs[:n_in]
    out_ref = refs[n_in]
    held = refs[n_in + 1 : 2 * n_in + 1]
    (
        left_ref,
        right_ref,
        part_ref,
        sums_ref,
        cells_first,
        cells_second,
        edge_first,
        edge_second,
        got_first,
        got_second,
        ring_ref,
        main_first,
        main_second,
        ends_first,
        ends_second,
        parts_ref,
        place_ref,
        final_ref,
        fetch_sem,
        part_sem,
        halo_sem,
        edge_sem,
    ) = refs[2 * n_in + 1 :]
    n_gx, n_gy, n_gz = sizes
    slab = n_gy * n_gz
    me = (lax.axis_index("gx"), lax.axis_index("gy"), lax.axis_index("gz"))
    mine = me[1] * n_gz + me[2]
    at_x = {d: (me[0] + d + n_gx) % n_gx for d in (-1, 0, 1)}
    at_y = [(me[1] + d) % n_gy for d in range(n_gy)]
    at_z = [(me[2] + d) % n_gz for d in range(n_gz)]

    def place(move):
        return (at_x[move[0]], at_y[move[1] % n_gy], at_z[move[2] % n_gz])

    others = [(dy, dz) for dy in range(n_gy) for dz in range(n_gz) if (dy, dz) != (0, 0)]

    fetches = [
        pltpu.make_async_copy(source, kept, fetch_sem.at[n])
        for n, (source, kept) in enumerate(zip(sources, held))
    ]
    for fetch in fetches[:4]:
        fetch.start()
    barrier = pltpu.get_barrier_semaphore()
    for da in (-1, 1):
        for db in (-1, 0, 1):
            for dc in (-1, 0, 1):
                pl.semaphore_signal(
                    barrier, inc=1, device_id=place((da, db, dc)), device_id_type=MESH
                )
    for dy, dz in others:
        pl.semaphore_signal(
            barrier, inc=1, device_id=(me[0], at_y[dy], at_z[dz]), device_id_type=MESH
        )
    for fetch in fetches[4:]:
        fetch.start()

    features, dest, cells, mass, style, *layers = held
    which = lax.broadcasted_iota(jnp.int32, (32, 2048), 0)
    spot = lax.broadcasted_iota(jnp.int32, (32, 2048), 1)
    wanted = (which % 16) * 128 + (which // 16) * 127
    pick = jnp.where(spot == wanted, 1.0, 0.0).astype(BF16)

    fetches[0].wait()
    for x in range(2):
        turned = jnp.transpose(features[:, x].astype(F32), (1, 0, 2))
        cells_first[1 + x, pl.ds(1, 8)] = turned.astype(BF16)
    pack_edges(cells_first, pick, edge_first)

    pl.semaphore_wait(barrier, slab - 1 + 18)

    def start_halo(layer, cells_ref, edge_ref, got_ref):
        for n, move in enumerate(SIDES):
            pltpu.make_async_remote_copy(
                src_ref=edge_ref,
                dst_ref=got_ref.at[n],
                send_sem=edge_sem.at[layer, 0],
                recv_sem=edge_sem.at[layer, 1],
                device_id=place(move),
                device_id_type=MESH,
            ).start()
        for da, db in PLANAR:
            group = 0 if da == 0 else 2
            src_x = {1: pl.ds(2, 1), -1: pl.ds(1, 1), 0: pl.ds(1, 2)}[da]
            dst_x = {1: pl.ds(0, 1), -1: pl.ds(3, 1), 0: pl.ds(1, 2)}[da]
            src_y = {1: pl.ds(8, 1), -1: pl.ds(1, 1), 0: pl.ds(1, 8)}[db]
            dst_y = {1: pl.ds(0, 1), -1: pl.ds(9, 1), 0: pl.ds(1, 8)}[db]
            pltpu.make_async_remote_copy(
                src_ref=cells_ref.at[src_x, src_y],
                dst_ref=cells_ref.at[dst_x, dst_y],
                send_sem=halo_sem.at[layer, group],
                recv_sem=halo_sem.at[layer, group + 1],
                device_id=place((da, db, 0)),
                device_id_type=MESH,
            ).start()

    def wait_for(ref, sem):
        pltpu.make_async_copy(ref, ref, sem).wait()

    def wait_beside(layer, cells_ref):
        four = cells_ref.at[pl.ds(0, 1), pl.ds(0, 4)]
        wait_for(four, halo_sem.at[layer, 1])

    def wait_across(layer, cells_ref):
        twenty = cells_ref.at[pl.ds(0, 2), pl.ds(0, 10)]
        wait_for(twenty, halo_sem.at[layer, 3])

    def wait_edges(layer, got_ref):
        wait_for(got_ref, edge_sem.at[layer, 1])

    def wait_sent(layer, cells_ref, got_ref):
        wait_for(cells_ref.at[pl.ds(0, 1), pl.ds(0, 4)], halo_sem.at[layer, 0])
        wait_for(cells_ref.at[pl.ds(0, 2), pl.ds(0, 10)], halo_sem.at[layer, 2])
        wait_for(got_ref, edge_sem.at[layer, 0])

    start_halo(0, cells_first, edge_first, got_first)
    for fetch in fetches[1:4]:
        fetch.wait()
    paint(dest[...], cells[...], mass[...], live_ref[0], left_ref, right_ref, part_ref)
    sums_ref[pl.ds(mine, 1)] = part_ref[pl.ds(mine, 1)]
    for dy, dz in others:
        pltpu.make_async_remote_copy(
            src_ref=part_ref.at[at_y[dy] * n_gz + at_z[dz]],
            dst_ref=sums_ref.at[mine],
            send_sem=part_sem.at[0],
            recv_sem=part_sem.at[1],
            device_id=(me[0], at_y[dy], at_z[dz]),
            device_id_type=MESH,
        ).start()


    nth = lax.broadcasted_iota(jnp.int32, (64, 256), 0) % 32
    lane = lax.broadcasted_iota(jnp.int32, (64, 256), 1)
    for pair in range(8):
        target = 128 * (nth % 2) + 127 * (nth // 16)
        hit = (nth % 16 // 2 == pair) & (lane == target)
        place_ref[pair] = jnp.where(hit, 1.0, 0.0).astype(BF16)
    for fetch in fetches[4:]:
        fetch.wait()
    style = style[...]
    modulate(layers[1], style, layers[0][...], main_first, ends_first)
    modulate(layers[5], style, layers[4][...], main_second, ends_second)
    bias_first, gain_first, bias_second, gain_second = (
        jnp.broadcast_to(column(layers[n][...]), (64, 128)) for n in (2, 3, 6, 7)
    )

    wait_beside(0, cells_first)
    convolve_own(cells_first, main_first, parts_ref)
    wait_edges(0, got_first)
    unpack_edges(got_first, ring_ref)
    convolve_ends(ring_ref, ends_first, main_first)
    rest = sums_ref.at[pl.ds(0, slab - 1)]
    wait_for(rest, part_sem.at[1])
    density = sums_ref[0].astype(F32)
    for n in range(1, slab):
        density = density + sums_ref[n].astype(F32)
    wait_across(0, cells_first)

    def keep(row, values):
        cells_second[1 + row // 8, 1 + row % 8] = activate(
            values + gain_first * density[row : row + 1] + bias_first
        ).astype(BF16)

    convolve_halo(cells_first, main_first, parts_ref, place_ref, keep)
    pack_edges(cells_second, pick, edge_second)
    start_halo(1, cells_second, edge_second, got_second)
    wait_beside(1, cells_second)
    convolve_own(cells_second, main_second, parts_ref)
    wait_edges(1, got_second)
    unpack_edges(got_second, ring_ref)
    convolve_ends(ring_ref, ends_second, main_second)
    wait_across(1, cells_second)

    def finish(row, values):
        final_ref[row // 8, row % 8] = activate(
            values + gain_second * density[row : row + 1] + bias_second
        )
        if row % 8 == 7:
            turned = jnp.transpose(final_ref[row // 8], (1, 0, 2))
            out_ref[:, row // 8] = turned.astype(BF16)

    convolve_halo(cells_second, main_second, parts_ref, place_ref, finish)
    wait_for(rest, part_sem.at[0])
    wait_sent(0, cells_first, got_first)
    wait_sent(1, cells_second, got_second)


def shards(sizes, features, dest, cells, masses, live, style, *layers):
    slab = sizes[1] * sizes[2]
    operands = [
        features,
        dest.reshape(1, -1),
        cells,
        masses,
        style.reshape(1, -1),
    ]
    for affine, kernel, bias, gain in (layers[:4], layers[4:]):
        operands += [affine.T, kernel, bias.reshape(1, -1), gain.reshape(1, -1)]
    operands = [pltpu.with_memory_space_constraint(x, pltpu.HBM) for x in operands]
    result = pl.pallas_call(
        functools.partial(body, sizes, len(operands)),
        out_shape=pltpu.VMEM((64, 2, 8, 128), BF16),
        in_specs=[pl.BlockSpec(memory_space=pltpu.SMEM)]
        + [pl.BlockSpec(memory_space=pltpu.HBM)] * len(operands),
        out_specs=pl.BlockSpec(memory_space=pltpu.VMEM),
        scratch_shapes=[pltpu.VMEM(x.shape, x.dtype) for x in operands]
        + [
            pltpu.VMEM((512, 2048), BF16),
            pltpu.VMEM((128, 2048), BF16),
            pltpu.VMEM((slab, 16, 128), BF16),
            pltpu.VMEM((slab, 16, 128), BF16),
            pltpu.VMEM((4, 10, 64, 128), BF16),
            pltpu.VMEM((4, 10, 64, 128), BF16),
            pltpu.VMEM((16, 128), BF16),
            pltpu.VMEM((16, 128), BF16),
            pltpu.VMEM((18, 16, 128), BF16),
            pltpu.VMEM((18, 16, 128), BF16),
            pltpu.VMEM((4, 16, 128), F32),
            pltpu.VMEM((192, 768), BF16),
            pltpu.VMEM((192, 768), BF16),
            pltpu.VMEM((128, 1152), BF16),
            pltpu.VMEM((128, 1152), BF16),
            pltpu.VMEM((8, 192, 256), F32),
            pltpu.VMEM((8, 64, 256), BF16),
            pltpu.VMEM((2, 8, 64, 128), F32),
            pltpu.SemaphoreType.DMA((len(operands),)),
            pltpu.SemaphoreType.DMA((2,)),
            pltpu.SemaphoreType.DMA((2, 4)),
            pltpu.SemaphoreType.DMA((2, 2)),
        ],
        compiler_params=pltpu.CompilerParams(
            collective_id=0, has_side_effects=True, vmem_limit_bytes=40 * 1024 * 1024
        ),
        name="styled_block",
    )(live, *operands)
    return result


def solution(mesh):
    sizes = (mesh.shape["gx"], mesh.shape["gy"], mesh.shape["gz"])
    spread = P(("gx", "gy", "gz"), None)
    return jax.shard_map(
        functools.partial(shards, sizes),
        mesh=mesh,
        in_specs=(P(None, "gx", "gy", "gz"), spread, spread, spread, P(("gx", "gy", "gz")))
        + (P(),) * 9,
        out_specs=P(None, "gx", "gy", "gz"),
        check_vma=False,
    )
```
